32 devices in a mesh: path: 8 (over z, x), mp: 4 (over y, core).
Axes of the slice: x: 2, y: 2, z: 4, core: 2. Of those that a mesh axis runs over, the one named last changes fastest.
Arguments:
- tokens: bfloat16 [3072, 2048], P('path', 'mp'), may hold values from -6 to 6
- cotangent: bfloat16 [3072, 2048], P('path', 'mp'), may hold values from -6 to 6
- path_weights: bfloat16 [8, 3, 4096, 2048], P('path', None, 'mp'), may hold values from -6 to 6
- outer_weights: float32 [8, 3, 2, 4, 128, 2048], P('path', None, None, 'mp'), may hold values from -6 to 6
- momentum: bfloat16 [8, 3, 2, 4, 128, 2048], P('path', None, None, 'mp'), may hold values from -6 to 6
- assignment: int32 [3, 8], replicated, may hold values from 0 to 1, as said below
- owners: int32 [3, 2, 8], replicated, may hold values from 0 to 7, each once within a row
Outputs:
- outputs: bfloat16 [3072, 2048], P('path', 'mp')
- refreshed: bfloat16 [8, 3, 2, 4, 128, 2048], P('path', None, None, 'mp')
The draws below stay inside these ranges and needn't reach their ends.
Inputs may be any that keep to these rules, and one draw needn't show every extreme that they name: `assignment`: every one of the 2 modules of a level is used by at least one path; how many paths share a module varies from module to module. For each level and module, the owners of its 8 pieces are the 8 path indices, each once.
All inputs are finite; a program needn't handle non-finite values.
Results may differ from the reference program's by a relative error of at most 0.0068.
Values may be sent and summed in bfloat16 or wider, within the bound.
No kernel may reach another device: no remote copies, remote signals or barrier semaphores. Data moves between devices by JAX's collectives and lax.ppermute only.
A program may use at most 128 MiB of HBM per device.

```python
import jax
import jax.numpy as jnp
from jax import lax

D = 2048
FF = 4096
ROWS = 384
LEVELS = 3
M = 2
TOKENS = 3072
B = 128
N_PATH = 8
N_MP = 4


def draw_assignment(key, part):
    rows = []
    for level in range(LEVELS):
        sub = jax.random.fold_in(key, 11 + level)
        first_key, pick_key, label_key, order_key = jax.random.split(sub, 4)
        first = jax.random.permutation(first_key, M).astype(jnp.int32)
        picks = jax.random.randint(pick_key, (3, N_PATH), 0, M)
        labels = jax.random.permutation(label_key, M).astype(jnp.int32)
        mixed = labels[jnp.min(picks, axis=0)]
        mixed = mixed.at[:M].set(first)
        rows.append(jax.random.permutation(order_key, mixed).astype(jnp.int32))
    return jnp.stack(rows).astype(jnp.int32)


def block_scale(own_key, extent, pieces, least, high):
    level, own = 1.0, jax.random.fold_in(own_key, 6)
    for dim, blocks in pieces:
        heights = jnp.exp(jax.random.uniform(jax.random.fold_in(own, dim), (blocks,), jnp.float32, least / len(pieces), high / len(pieces)))
        level = level * jnp.repeat(heights, extent[dim] // blocks).reshape([-1 if axis == dim else 1 for axis in range(len(extent))])
    return level


def bell_draw(own_key, shape, spread, limit, pieces=(), kind=jnp.bfloat16):
    factor_of = block_scale(own_key, shape, pieces, -0.22, 0.18) if pieces else 1.0
    result = jax.random.normal(own_key, shape, jnp.float32) * spread * factor_of
    return jnp.minimum(jnp.maximum(result, -limit), limit).astype(kind)


def setup_inputs(seed: int = 0) -> dict:
    seeds = jax.random.split(jax.random.key(seed), 8)
    tokens = bell_draw(seeds[0], (TOKENS, D), 1.0, 6.0, ((0, 8), (1, 4)))
    cotangent = bell_draw(seeds[1], (TOKENS, D), 1.0, 6.0, ((0, 8), (1, 4)))
    path_weights = bell_draw(seeds[2], (N_PATH, LEVELS, FF, D), 1.0, 6.0, ((0, 8), (2, 4)))
    outer_weights = bell_draw(seeds[3], (N_PATH, LEVELS, M, N_MP, B, D), 1.0, 6.0, ((0, 8), (3, 4)), jnp.float32)
    momentum = bell_draw(seeds[4], (N_PATH, LEVELS, M, N_MP, B, D), 1.0, 6.0, ((0, 8), (3, 4)))
    assignment = draw_assignment(jax.random.fold_in(seeds[7], 71), 0)
    owners = jax.vmap(lambda own: jax.random.permutation(own, N_PATH))(jax.random.split(seeds[6], LEVELS * M)).reshape((LEVELS, M, N_PATH)).astype(jnp.int32)
    return {"tokens": tokens, "cotangent": cotangent, "path_weights": path_weights, "outer_weights": outer_weights, "momentum": momentum, "assignment": assignment, "owners": owners}


mu_outer = 0.9
eta_outer = 0.7
lr_inner = 2.0


def contract(left, right, left_dim, right_dim):
    return lax.dot_general(left, right, (((left_dim,), (right_dim,)), ((), ())), preferred_element_type=jnp.float32)


def inner_final(inputs, upstream, weights):
    scale_d = D ** -0.5
    scale_f = FF ** -0.5
    gate = contract(inputs, weights[0], 1, 1) * scale_d
    upper = contract(inputs, weights[1], 1, 1) * scale_d
    sig = jax.nn.sigmoid(gate)
    act = gate * sig
    hidden = (act * upper).astype(jnp.bfloat16)
    grad_down = contract(hidden, upstream, 0, 0) * scale_f
    grad_hidden = contract(upstream, weights[2], 1, 1) * scale_f
    pre_gate = (grad_hidden * upper * sig * (1.0 + gate * (1.0 - sig))).astype(jnp.bfloat16)
    pre_up = (grad_hidden * act).astype(jnp.bfloat16)
    grad_gate = contract(pre_gate, inputs, 0, 0) * scale_d
    grad_up = contract(pre_up, inputs, 0, 0) * scale_d
    grads = jnp.stack([grad_gate, grad_up, grad_down])
    return weights.astype(jnp.float32) - lr_inner * grads


def to_full(stored, owner_row):
    placed = stored[owner_row]
    return jnp.transpose(placed, (1, 0, 2, 3)).reshape(FF, D)


def to_owner(full, owner_row):
    blocks = full.reshape(N_MP, N_PATH, -1, D)
    inverse = jnp.argsort(owner_row).astype(jnp.int32)
    return jnp.transpose(blocks[:, inverse], (1, 0, 2, 3))


def reference(tokens, cotangent, path_weights, outer_weights, momentum, assignment, owners):
    level_ids = jnp.arange(LEVELS, dtype=jnp.int32)

    def add_path(total, index):
        inputs = lax.dynamic_slice_in_dim(tokens, index * ROWS, ROWS, 0)
        upstream = lax.dynamic_slice_in_dim(cotangent, index * ROWS, ROWS, 0)
        final = inner_final(inputs, upstream, path_weights[index])
        return total.at[level_ids, assignment[:, index]].add(final), None

    totals, _ = lax.scan(add_path, jnp.zeros((LEVELS, M, FF, D), jnp.float32), jnp.arange(N_PATH, dtype=jnp.int32))
    table = (assignment[:, None, :] == jnp.arange(M, dtype=jnp.int32)[None, :, None]).astype(jnp.float32)
    shares = jnp.sum(table, axis=2)
    full_outer = jax.vmap(jax.vmap(to_full))(jnp.moveaxis(outer_weights, 0, 2), owners)
    full_mom = jax.vmap(jax.vmap(to_full))(jnp.moveaxis(momentum, 0, 2), owners).astype(jnp.float32)
    mean = totals / shares[:, :, None, None]
    delta = full_outer - mean
    velocity = mu_outer * full_mom + delta
    fresh = (full_outer - eta_outer * (delta + mu_outer * velocity)).astype(jnp.bfloat16)
    refreshed = jnp.moveaxis(jax.vmap(jax.vmap(to_owner))(fresh, owners), 2, 0)

    def forward(index):
        inputs = lax.dynamic_slice_in_dim(tokens, index * ROWS, ROWS, 0)
        weights = fresh[level_ids, assignment[:, index]]
        gate = contract(inputs, weights[0], 1, 1) * (D ** -0.5)
        upper = contract(inputs, weights[1], 1, 1) * (D ** -0.5)
        hidden = (gate * jax.nn.sigmoid(gate) * upper).astype(jnp.bfloat16)
        return (contract(hidden, weights[2], 1, 0) * (FF ** -0.5)).astype(jnp.bfloat16)

    outputs = lax.map(forward, jnp.arange(N_PATH, dtype=jnp.int32)).reshape(N_PATH * ROWS, D)
    return outputs, refreshed
```

```python
import functools

import jax
import jax.numpy as jnp
from jax import lax
from jax.experimental import pallas as pl
from jax.experimental.pallas import tpu as pltpu
from jax.sharding import PartitionSpec as P

mu_outer = 0.9
eta_outer = 0.7
lr_inner = 2.0

STREAMS = 2
FOLD = 2


def contract(left, right, left_dim, right_dim):
    return lax.dot_general(
        left, right, (((left_dim,), (right_dim,)), ((), ())), preferred_element_type=jnp.float32
    )


def params():
    return pltpu.CompilerParams(vmem_limit_bytes=56 * 2**20)


def front_kernel(scale_d, scale_f, x_ref, c_ref, gate_ref, up_ref, down_ref, hidden_ref, pre_gate_ref, pre_up_ref):
    gate = contract(gate_ref[0, 0], x_ref[...], 1, 1) * scale_d
    upper = contract(up_ref[0, 0], x_ref[...], 1, 1) * scale_d
    grad = contract(down_ref[0, 0], c_ref[...], 1, 1) * scale_f
    sig = jax.nn.sigmoid(gate)
    act = gate * sig
    hidden_ref[...] = (act * upper).astype(jnp.bfloat16)
    pre_gate_ref[...] = (grad * upper * sig * (1.0 + gate * (1.0 - sig))).astype(jnp.bfloat16)
    pre_up_ref[...] = (grad * act).astype(jnp.bfloat16)


def front(inputs, upstream, weights, scale_d, scale_f):
    rows, width = inputs.shape
    units = weights.shape[2]
    tile = min(256, units)
    whole = pl.BlockSpec((rows, width), lambda i: (0, 0))
    return pl.pallas_call(
        functools.partial(front_kernel, scale_d, scale_f),
        grid=(units // tile,),
        in_specs=[whole, whole]
        + [pl.BlockSpec((1, 1, tile, width), lambda i, level=level: (0, level, i, 0)) for level in range(3)],
        out_specs=[pl.BlockSpec((tile, rows), lambda i: (i, 0))] * 3,
        out_shape=[jax.ShapeDtypeStruct((units, rows), jnp.bfloat16)] * 3,
        compiler_params=params(),
        cost_estimate=pl.CostEstimate(
            flops=6 * rows * width * units,
            bytes_accessed=6 * units * width + 4 * rows * width + 6 * units * rows,
            transcendentals=units * rows,
        ),
    )(inputs, upstream, weights, weights, weights)


def finals_kernel(scale, block, pieces, table_ref, left_ref, right_ref, weight_ref, own_ref, send_ref):
    grad = contract(left_ref[...], right_ref[...], 1, 0) * (lr_inner * scale)
    for q in range(pieces):
        rows = slice(q * block, (q + 1) * block)
        final = weight_ref[0, 0, rows, :].astype(jnp.float32) - grad[rows]
        spot = table_ref[1, q]

        @pl.when(table_ref[0, q] == 0)
        def _():
            own_ref[spot] = final

        @pl.when(table_ref[0, q] != 0)
        def _():
            send_ref[spot] = final.astype(jnp.bfloat16)


def finals(table, left, right, weights, level, columns, scale, line, block):
    start, tiles, tile = columns
    units, rows = left.shape
    spec = pl.BlockSpec((line, block, tile), lambda t, table: (0, 0, t))
    width = tiles * tile
    shape = (line, block, width)
    return pl.pallas_call(
        functools.partial(finals_kernel, scale, block, units // block),
        grid_spec=pltpu.PrefetchScalarGridSpec(
            num_scalar_prefetch=1,
            grid=(tiles,),
            in_specs=[
                pl.BlockSpec((units, rows), lambda t, table: (0, 0)),
                pl.BlockSpec((rows, tile), lambda t, table: (0, start(t))),
                pl.BlockSpec((1, 1, units, tile), lambda t, table: (0, level, 0, start(t))),
            ],
            out_specs=[spec, spec],
        ),
        out_shape=[jax.ShapeDtypeStruct(shape, jnp.float32), jax.ShapeDtypeStruct(shape, jnp.bfloat16)],
        compiler_params=params(),
        cost_estimate=pl.CostEstimate(
            flops=2 * rows * width * units, bytes_accessed=5 * units * width + 2 * units * rows, transcendentals=0
        ),
    )(table, left, right, weights)


def product(x_ref, parts):
    total = None
    at = 0
    for part in parts:
        width = part.shape[2]
        value = contract(part[...].reshape(-1, width), x_ref[:, at : at + width], 1, 1)
        total = value if total is None else total + value
        at += width
    return total


def gate_kernel(scale, block, line, table_ref, x_ref, *refs):
    out_ref = refs[-1]
    count = (len(refs) - 1) // 2
    for side, parts in enumerate((refs[:count], refs[count:-1])):
        value = product(x_ref, parts) * scale
        for r in range(line):
            out_ref[table_ref[0, side * line + r]] = value[r * block : (r + 1) * block]


def hidden_kernel(scale, block, line, table_ref, x_ref, gate_ref, *refs):
    out_ref = refs[-1]
    count = (len(refs) - 1) // 2
    for side, parts in enumerate((refs[:count], refs[count:-1])):
        value = product(x_ref, parts) * scale
        for r in range(line):
            gate = gate_ref[table_ref[0, side * line + r]]
            upper = value[r * block : (r + 1) * block]
            hidden = gate * jax.nn.sigmoid(gate) * upper
            out_ref[table_ref[1, side * line + r]] = hidden.astype(jnp.bfloat16)


def forward(kernel, table, inputs, extra, parts, dtype, scale, line, block):
    rows = inputs.shape[0]
    pieces = 2 * line
    vmem = pl.BlockSpec(memory_space=pltpu.VMEM)
    return pl.pallas_call(
        functools.partial(kernel, scale, block, line),
        in_specs=[pl.BlockSpec(memory_space=pltpu.SMEM)] + [vmem] * (1 + len(extra) + len(parts)),
        out_specs=vmem,
        out_shape=jax.ShapeDtypeStruct((pieces, block, rows), dtype),
        compiler_params=params(),
        cost_estimate=pl.CostEstimate(
            flops=2 * rows * inputs.shape[1] * pieces * block,
            bytes_accessed=2 * inputs.shape[1] * pieces * block,
            transcendentals=0,
        ),
    )(table, inputs, *extra, *parts)


def down_kernel(scale, left_ref, near_ref, far_ref, out_ref):
    half = left_ref.shape[1] // 2
    width = near_ref.shape[2]
    total = contract(left_ref[:, :half], near_ref[...].reshape(-1, width), 1, 0)
    total = total + contract(left_ref[:, half:], far_ref[...].reshape(-1, width), 1, 0)
    out_ref[...] = total * scale


def down(left, near, far, scale):
    rows, units = left.shape
    line, block, width = near.shape
    tile = width
    spec = pl.BlockSpec((line, block, tile), lambda t: (0, 0, t))
    return pl.pallas_call(
        functools.partial(down_kernel, scale),
        grid=(width // tile,),
        in_specs=[pl.BlockSpec((rows, units), lambda t: (0, 0)), spec, spec],
        out_specs=pl.BlockSpec((rows, tile), lambda t: (0, t)),
        out_shape=jax.ShapeDtypeStruct((rows, width), jnp.float32),
        compiler_params=params(),
        cost_estimate=pl.CostEstimate(
            flops=2 * rows * width * units, bytes_accessed=2 * units * width + 4 * rows * width, transcendentals=0
        ),
    )(left, near, far)


def pairs_of(size, bit):
    return [(i, i ^ bit) for i in range(size)]


def gather_mp(value, size, index):
    parts = [value]
    bit = size // 2
    while bit:
        sent = jnp.concatenate(parts, axis=1)
        got = lax.ppermute(sent, "mp", pairs_of(size, bit))
        high = (index & bit) != 0
        width = value.shape[1]
        merged = []
        for i, part in enumerate(parts):
            other = got[:, i * width : (i + 1) * width]
            merged += [jnp.where(high, other, part), jnp.where(high, part, other)]
        parts = merged
        bit //= 2
    return jnp.concatenate(parts, axis=1)


def scatter_mp(value, size, index):
    width = value.shape[1] // size
    parts = [value[:, i * width : (i + 1) * width] for i in range(size)]
    bit = 1
    while bit < size:
        high = (index & bit) != 0
        keep = [jnp.where(high, parts[i + 1], parts[i]) for i in range(0, len(parts), 2)]
        sent = [jnp.where(high, parts[i], parts[i + 1]) for i in range(0, len(parts), 2)]
        got = lax.ppermute(jnp.concatenate(sent, axis=1), "mp", pairs_of(size, bit))
        parts = [part + got[:, i * width : (i + 1) * width] for i, part in enumerate(keep)]
        bit *= 2
    return parts[0]


def shards(tokens, cotangent, path_weights, outer_weights, momentum, assignment, owners):
    paths = lax.axis_size("path")
    ranks = lax.axis_size("mp")
    line = paths // FOLD
    me = lax.axis_index("path")
    rank = lax.axis_index("mp")
    z, side = me // FOLD, me % FOLD
    levels, units, width = path_weights.shape[1:]
    modules, block = outer_weights.shape[2], outer_weights.shape[4]
    scale_d = width ** (-0.5)
    scale_f = (units * ranks) ** (-0.5)

    module_ids = jnp.arange(modules, dtype=jnp.int32)
    path_ids = jnp.arange(paths, dtype=jnp.int32)
    mine = lax.dynamic_index_in_dim(assignment, me, 1, keepdims=False)
    theirs = lax.dynamic_index_in_dim(assignment, me ^ 1, 1, keepdims=False)
    is_mine = mine[:, None] == module_ids[None, :]
    is_theirs = theirs[:, None] == module_ids[None, :]
    shares = jnp.sum((assignment[:, None, :] == module_ids[None, :, None]).astype(jnp.float32), axis=2)
    owner_rows = jnp.sum(jnp.where(is_mine[:, :, None], owners, 0), axis=1)
    apart = (owner_rows % FOLD) ^ side
    leaves = jnp.stack([apart, owner_rows // FOLD], axis=1)
    slot = apart * line + (z - owner_rows // FOLD + line) % line
    piece_at = jnp.sum(
        jnp.where(slot[:, None, :] == path_ids[None, :, None], path_ids[None, None, :], 0), axis=2
    )
    down_at = jnp.sum(
        jnp.where(piece_at[1][:, None] == path_ids[None, :], slot[2][None, :], 0), axis=1
    )
    gate_table = piece_at[0][None]
    hidden_table = jnp.stack([piece_at[1], down_at])

    right = [(i, i + FOLD) for i in range(paths - FOLD)]
    left = [(i + FOLD, i) for i in range(paths - FOLD)]
    across = pairs_of(paths, 1)

    def permute(value, pairs):
        return lax.ppermute(value, "path", pairs)

    half = width // STREAMS
    narrow = width // (ranks * STREAMS)

    def ranges(level, s):
        if level == 2:
            return [(j * narrow * STREAMS + s * narrow, narrow) for j in range(ranks)]
        return [(s * half, half)]

    def columns(level, s):
        if level == 2:
            return (lambda t: t * STREAMS + s), ranks, narrow
        tile = min(512, half)
        return (lambda t: s * (half // tile) + t), half // tile, tile

    def cut(array, level, s):
        parts = [array[..., at : at + size] for at, size in ranges(level, s)]
        return parts[0] if len(parts) == 1 else jnp.concatenate(parts, axis=-1)

    inputs = gather_mp(tokens, ranks, rank)
    upstream = gather_mp(cotangent, ranks, rank)
    hidden, pre_gate, pre_up = front(inputs, upstream, path_weights, scale_d, scale_f)
    sources = ((pre_gate, inputs, scale_d), (pre_up, inputs, scale_d), (hidden, upstream, scale_f))

    zeros = jnp.zeros((modules, block, half), jnp.bfloat16)
    flow = [[zeros, zeros] for _ in range(STREAMS)]
    waiting = [None] * STREAMS
    near = [[None] * STREAMS for _ in range(levels)]
    far = [[None] * STREAMS for _ in range(levels)]
    fresh_all = [[None] * STREAMS for _ in range(levels)]

    def term(own, got, level, at, live):
        kept = lax.dynamic_index_in_dim(own, at, 0, keepdims=True)
        come = lax.dynamic_index_in_dim(got, at, 0, keepdims=True).astype(jnp.float32)
        a = (is_mine[level] & live)[:, None, None]
        b = (is_theirs[level] & live)[:, None, None]
        return jnp.where(a, kept, 0.0) + jnp.where(b, come, 0.0)

    def deliver(level, s, seen):
        fresh, rights, lefts = seen
        ring = [fresh] + [
            jnp.where(z >= r, rights[r - 1], lefts[line - 1 - r]) for r in range(1, line)
        ]
        pick = lambda m: jnp.stack([lax.dynamic_index_in_dim(a, m, 0, keepdims=False) for a in ring])
        near[level][s] = pick(mine[level])
        far[level][s] = permute(pick(theirs[level]), across)

    def round_(level, s):
        if level < levels:
            source = sources[level]
            own, send = finals(
                leaves[level], source[0], source[1], path_weights, level, columns(level, s), source[2], line, block
            )
            got = permute(send, across)
        for step in range(1, line):
            moved = []
            for way, pairs in enumerate((right, left)):
                value = flow[s][way]
                if level < levels:
                    at = line - step + z if way == 0 else z - line + step
                    live = z < step if way == 0 else z >= line - step
                    value = value.astype(jnp.float32) + term(own, got, level, jnp.clip(at, 0, line - 1), live)
                    value = value.astype(jnp.bfloat16)
                elif step == line - 1:
                    break
                moved.append(permute(value, pairs))
            if moved:
                flow[s] = moved
            if waiting[s] is not None:
                if step < line - 1:
                    waiting[s][1].append(moved[0])
                    waiting[s][2].append(moved[1])
                if step == max(line - 2, 1):
                    deliver(level - 1, s, waiting[s])
        if level < levels:
            sums = term(own, got, level, z, True) + flow[s][0].astype(jnp.float32) + flow[s][1].astype(jnp.float32)
            stored = cut(outer_weights[0, level, :, 0], level, s)
            old = cut(momentum[0, level, :, 0], level, s).astype(jnp.float32)
            delta = stored - sums / shares[level][:, None, None]
            velocity = mu_outer * old + delta
            fresh = (stored - eta_outer * (delta + mu_outer * velocity)).astype(jnp.bfloat16)
            fresh_all[level][s] = fresh
            flow[s] = [permute(fresh, right), permute(fresh, left)]
            waiting[s] = (fresh, [flow[s][0]], [flow[s][1]])

    gate_new = hidden_new = None
    outs = []
    for level in range(levels + 1):
        for s in range(STREAMS):
            round_(level, s)
            if level == 3:
                total = down(hidden_new, near[2][s], far[2][s], scale_f)
                outs.append(scatter_mp(total, ranks, rank))
        if level == 1:
            gate_new = forward(
                gate_kernel, gate_table, inputs, (), near[0] + far[0], jnp.float32, scale_d, line, block
            )
        if level == 2:
            value = forward(
                hidden_kernel, hidden_table, inputs, (gate_new,), near[1] + far[1], jnp.bfloat16, scale_d, line, block
            )
            hidden_new = value.reshape(units, -1).T

    outputs = jnp.concatenate(outs, axis=1).astype(jnp.bfloat16)
    rows = []
    for level in range(levels):
        parts = {}
        for s in range(STREAMS):
            at = 0
            for start, size in ranges(level, s):
                parts[start] = fresh_all[level][s][..., at : at + size]
                at += size
        rows.append(jnp.concatenate([parts[k] for k in sorted(parts)], axis=-1))
    refreshed = jnp.stack(rows).reshape(1, levels, modules, 1, block, width)
    return outputs, refreshed


def solution(mesh):
    return jax.shard_map(
        shards,
        mesh=mesh,
        in_specs=(
            P("path", "mp"),
            P("path", "mp"),
            P("path", None, "mp", None),
            P("path", None, None, "mp", None, None),
            P("path", None, None, "mp", None, None),
            P(),
            P(),
        ),
        out_specs=(P("path", "mp"), P("path", None, None, "mp", None, None)),
        check_vma=False,
    )
```

```python
import functools

import jax
import jax.numpy as jnp
from jax import lax
from jax.experimental import pallas as pl
from jax.experimental.pallas import tpu as pltpu
from jax.sharding import PartitionSpec as P

mu_outer = 0.9
eta_outer = 0.7
lr_inner = 2.0

STREAMS = 2
FOLD = 2


def contract(left, right, left_dim, right_dim):
    return lax.dot_general(
        left, right, (((left_dim,), (right_dim,)), ((), ())), preferred_element_type=jnp.float32
    )


def params(mib):
    return pltpu.CompilerParams(vmem_limit_bytes=mib * 2**20)


def spread(position, left, right_ref, chunks):
    size = left.shape[1] // chunks
    total = None
    for j in range(chunks):
        value = contract(left[:, j * size : (j + 1) * size], right_ref[position(j)], 1, 1)
        total = value if total is None else total + value
    return total


def open_kernel(scale, chunks, order_ref, x_ref, gate_w_ref, up_w_ref, gate_ref, up_ref, hidden_ref):
    position = lambda j: order_ref[j]
    gate = spread(position, gate_w_ref[0, 0], x_ref, chunks) * scale
    upper = spread(position, up_w_ref[0, 0], x_ref, chunks) * scale
    gate_ref[...] = gate
    up_ref[...] = upper
    hidden_ref[...] = (gate * jax.nn.sigmoid(gate) * upper).astype(jnp.bfloat16)


def close_kernel(scale, chunks, order_ref, c_ref, weight_ref, gate_ref, up_ref, pre_gate_ref, pre_up_ref):
    grad = spread(lambda j: order_ref[j], weight_ref[0, 0], c_ref, chunks) * scale
    gate, upper = gate_ref[...], up_ref[...]
    sig = jax.nn.sigmoid(gate)
    act = gate * sig
    pre_gate_ref[...] = (grad * upper * sig * (1.0 + gate * (1.0 - sig))).astype(jnp.bfloat16)
    pre_up_ref[...] = (grad * act).astype(jnp.bfloat16)


def front(kernel, scale, order, right, weights, picked, extra, dtypes):
    chunks, rows, size = right.shape
    units, width = weights.shape[2:]
    tile = min(256, units)
    thin = pl.BlockSpec((tile, rows), lambda i, order: (i, 0))
    return pl.pallas_call(
        functools.partial(kernel, scale, chunks),
        grid_spec=pltpu.PrefetchScalarGridSpec(
            num_scalar_prefetch=1,
            grid=(units // tile,),
            in_specs=[pl.BlockSpec((chunks, rows, size), lambda i, order: (0, 0, 0))]
            + [
                pl.BlockSpec((1, 1, tile, width), lambda i, order, level=level: (0, level, i, 0))
                for level in picked
            ]
            + [thin] * len(extra),
            out_specs=[thin] * len(dtypes),
        ),
        out_shape=[jax.ShapeDtypeStruct((units, rows), dtype) for dtype in dtypes],
        compiler_params=params(32),
        cost_estimate=pl.CostEstimate(
            flops=2 * len(picked) * rows * width * units,
            bytes_accessed=2 * len(picked) * units * width,
            transcendentals=units * rows,
        ),
    )(order, right, *[weights] * len(picked), *extra)


def finals_kernel(scale, block, pieces, table_ref, left_ref, right_ref, weight_ref, *refs):
    own_ref, send_ref = refs[-2:]
    grad = contract(left_ref[...], right_ref[0], 1, 0) * (lr_inner * scale)
    for q in range(pieces):
        rows = slice(q * block, (q + 1) * block)
        final = weight_ref[0, 0, rows, :].astype(jnp.float32) - grad[rows]
        spot = table_ref[1, q]

        @pl.when(table_ref[0, q] == 0)
        def _():
            own_ref[spot] = final

        @pl.when(table_ref[0, q] != 0)
        def _():
            send_ref[spot] = final.astype(jnp.bfloat16)


def finals(table, order, left, right, weights, level, columns, scale, line, block, after):
    start, tiles, tile = columns
    units, rows = left.shape
    per = right.shape[2] // tile
    spec = pl.BlockSpec((line, block, tile), lambda t, table, order: (0, 0, t))
    width = tiles * tile
    shape = (line, block, width)

    def kernel(table_ref, order_ref, *refs):
        finals_kernel(scale, block, units // block, table_ref, *refs)

    return pl.pallas_call(
        kernel,
        grid_spec=pltpu.PrefetchScalarGridSpec(
            num_scalar_prefetch=2,
            grid=(tiles,),
            in_specs=[
                pl.BlockSpec((units, rows), lambda t, table, order: (0, 0)),
                pl.BlockSpec(
                    (1, rows, tile), lambda t, table, order: (order[start(t) // per], 0, start(t) % per)
                ),
                pl.BlockSpec((1, 1, units, tile), lambda t, table, order: (0, level, 0, start(t))),
            ]
            + [pl.BlockSpec(memory_space=pl.ANY)] * len(after),
            out_specs=[spec, spec],
        ),
        out_shape=[jax.ShapeDtypeStruct(shape, jnp.float32), jax.ShapeDtypeStruct(shape, jnp.bfloat16)],
        compiler_params=params(24),
        cost_estimate=pl.CostEstimate(
            flops=2 * rows * width * units, bytes_accessed=5 * units * width + 2 * units * rows, transcendentals=0
        ),
    )(table, order, left, right, weights, *after)


def places(line, step):
    ups = lambda at: jnp.clip(line - step + at[2], 0, line - 1)
    downs = lambda at: jnp.clip(at[2] - line + step, 0, line - 1)
    return ups, downs


def running_kernel(line, step, at_ref, *refs):
    own_refs, got_refs, flow_refs, out_refs = refs[:2], refs[2:4], refs[4:-2], refs[-2:]
    modules = out_refs[0].shape[0]
    z = at_ref[2]
    lives = (z < step, z >= line - step)
    for way in range(2):
        for m in range(modules):
            total = jnp.where(lives[way] & (at_ref[0] == m), own_refs[way][0], 0.0)
            total = total + jnp.where(
                lives[way] & (at_ref[1] == m), got_refs[way][0].astype(jnp.float32), 0.0
            )
            if flow_refs:
                total = total + flow_refs[way][m].astype(jnp.float32)
            out_refs[way][m] = total.astype(jnp.bfloat16)


def running(at, own, got, flow, modules, step):
    line, block, width = own.shape
    tile = min(512, width)
    ups, downs = places(line, step)
    one = [
        pl.BlockSpec((1, block, tile), lambda t, at, spot=spot: (spot(at), 0, t)) for spot in (ups, downs)
    ]
    wide = pl.BlockSpec((modules, block, tile), lambda t, at: (0, 0, t))
    return pl.pallas_call(
        functools.partial(running_kernel, line, step),
        grid_spec=pltpu.PrefetchScalarGridSpec(
            num_scalar_prefetch=1,
            grid=(width // tile,),
            in_specs=one + one + [wide] * len(flow),
            out_specs=[wide, wide],
        ),
        out_shape=[jax.ShapeDtypeStruct((modules, block, width), jnp.bfloat16)] * 2,
        compiler_params=params(12),
        cost_estimate=pl.CostEstimate(
            flops=12 * modules * block * width, bytes_accessed=20 * block * width, transcendentals=0
        ),
    )(at, own, own, got, got, *flow)


def update_kernel(count, at_ref, share_ref, own_ref, got_ref, up_ref, low_ref, stored_ref, old_ref, *refs):
    fresh_ref, whole_ref = refs[-2:]
    for m in range(count):
        total = jnp.where(at_ref[0] == m, own_ref[0], 0.0)
        total = total + jnp.where(at_ref[1] == m, got_ref[0].astype(jnp.float32), 0.0)
        total = total + up_ref[m].astype(jnp.float32) + low_ref[m].astype(jnp.float32)
        stored = stored_ref[0, 0, m, 0]
        delta = stored - total / share_ref[m]
        velocity = mu_outer * old_ref[0, 0, m, 0].astype(jnp.float32) + delta
        fresh = (stored - eta_outer * (delta + mu_outer * velocity)).astype(jnp.bfloat16)
        fresh_ref[m] = fresh
        whole_ref[0, 0, m, 0] = fresh


def update(at, share, own, got, flow, outer_weights, momentum, whole, level, columns, after):
    start, tiles, tile = columns
    modules, block = outer_weights.shape[2], outer_weights.shape[4]
    one = pl.BlockSpec((1, block, tile), lambda t, at: (at[2], 0, t))
    wide = pl.BlockSpec((modules, block, tile), lambda t, at: (0, 0, t))
    state = pl.BlockSpec((1, 1, modules, 1, block, tile), lambda t, at: (0, level, 0, 0, 0, start(t)))
    extra = ([] if whole is None else [whole]) + after
    return pl.pallas_call(
        functools.partial(update_kernel, modules),
        grid_spec=pltpu.PrefetchScalarGridSpec(
            num_scalar_prefetch=1,
            grid=(tiles,),
            in_specs=[pl.BlockSpec(memory_space=pltpu.SMEM), one, one, wide, wide, state, state]
            + [pl.BlockSpec(memory_space=pl.ANY)] * len(extra),
            out_specs=[wide, state],
        ),
        out_shape=[
            jax.ShapeDtypeStruct((modules, block, tiles * tile), jnp.bfloat16),
            jax.ShapeDtypeStruct(outer_weights.shape, jnp.bfloat16),
        ],
        input_output_aliases={} if whole is None else {8: 1},
        compiler_params=params(16),
        cost_estimate=pl.CostEstimate(
            flops=12 * modules * block * tiles * tile,
            bytes_accessed=16 * modules * block * tiles * tile,
            transcendentals=0,
        ),
    )(at, share, own, got, *flow, outer_weights, momentum, *extra)


def deliver_kernel(line, at_ref, fresh_ref, *refs):
    ups, lows = refs[: line - 1], refs[line - 1 : 2 * line - 2]
    near_ref, far_ref, sems = refs[-3:]
    z = at_ref[2]
    for side, out_ref in enumerate((near_ref, far_ref)):
        module = at_ref[side]

        def copy(source, r, side=side, out_ref=out_ref, module=module):
            return pltpu.make_async_copy(source.at[module], out_ref.at[r], sems.at[side, r])

        copy(fresh_ref, 0).start()
        for r in range(1, line):

            @pl.when(z >= r)
            def _():
                copy(ups[r - 1], r).start()

            @pl.when(z < r)
            def _():
                copy(lows[line - 1 - r], r).start()

    for side, out_ref in enumerate((near_ref, far_ref)):
        for r in range(line):
            pltpu.make_async_copy(fresh_ref.at[0], out_ref.at[r], sems.at[side, r]).wait()


def deliver(at, fresh, ups, lows, after):
    line = len(ups) + 1
    shape = jax.ShapeDtypeStruct((line,) + fresh.shape[1:], fresh.dtype)
    anywhere = pl.BlockSpec(memory_space=pl.ANY)
    return pl.pallas_call(
        functools.partial(deliver_kernel, line),
        in_specs=[pl.BlockSpec(memory_space=pltpu.SMEM)] + [anywhere] * (2 * line - 1 + len(after)),
        out_specs=[pl.BlockSpec(memory_space=pltpu.VMEM)] * 2,
        out_shape=[shape, shape],
        scratch_shapes=[pltpu.SemaphoreType.DMA((2, line))],
        compiler_params=params(12),
        cost_estimate=pl.CostEstimate(
            flops=0, bytes_accessed=4 * shape.size * 2, transcendentals=0
        ),
    )(at, fresh, *ups, *lows, *after)


def product(order_ref, x_ref, parts):
    total = None
    size = x_ref.shape[2]
    at = 0
    for part in parts:
        for i in range(part.shape[2] // size):
            left = part[:, :, i * size : (i + 1) * size].reshape(-1, size)
            value = contract(left, x_ref[order_ref[at]], 1, 1)
            total = value if total is None else total + value
            at += 1
    return total


def gate_kernel(scale, block, line, order_ref, table_ref, x_ref, *refs):
    out_ref = refs[-1]
    count = (len(refs) - 1) // 2
    for side, parts in enumerate((refs[:count], refs[count:-1])):
        value = product(order_ref, x_ref, parts) * scale
        for r in range(line):
            out_ref[table_ref[0, side * line + r]] = value[r * block : (r + 1) * block]


def hidden_kernel(scale, block, line, order_ref, table_ref, x_ref, gate_ref, *refs):
    out_ref = refs[-1]
    count = (len(refs) - 1) // 2
    for side, parts in enumerate((refs[:count], refs[count:-1])):
        value = product(order_ref, x_ref, parts) * scale
        for r in range(line):
            gate = gate_ref[table_ref[0, side * line + r]]
            upper = value[r * block : (r + 1) * block]
            hidden = gate * jax.nn.sigmoid(gate) * upper
            out_ref[table_ref[1, side * line + r]] = hidden.astype(jnp.bfloat16)


def forward(kernel, order, table, inputs, extra, parts, dtype, scale, line, block):
    chunks, rows, size = inputs.shape
    pieces = 2 * line
    smem = pl.BlockSpec(memory_space=pltpu.SMEM)
    vmem = pl.BlockSpec(memory_space=pltpu.VMEM)
    return pl.pallas_call(
        functools.partial(kernel, scale, block, line),
        in_specs=[smem, smem] + [vmem] * (1 + len(extra) + len(parts)),
        out_specs=vmem,
        out_shape=jax.ShapeDtypeStruct((pieces, block, rows), dtype),
        compiler_params=params(32),
        cost_estimate=pl.CostEstimate(
            flops=2 * rows * chunks * size * pieces * block,
            bytes_accessed=2 * chunks * size * pieces * block,
            transcendentals=0,
        ),
    )(order, table, inputs, *extra, *parts)


def down_kernel(scale, left_ref, near_ref, far_ref, out_ref):
    line, block, width = near_ref.shape
    rows = left_ref.shape[2]
    near_left = left_ref[:line].reshape(line * block, rows)
    far_left = left_ref[line:].reshape(line * block, rows)
    total = contract(near_left, near_ref[...].reshape(-1, width), 0, 0)
    total = total + contract(far_left, far_ref[...].reshape(-1, width), 0, 0)
    out_ref[...] = total * scale


def down(left, near, far, scale):
    pieces, block, rows = left.shape
    width = near.shape[2]
    vmem = pl.BlockSpec(memory_space=pltpu.VMEM)
    return pl.pallas_call(
        functools.partial(down_kernel, scale),
        in_specs=[vmem] * 3,
        out_specs=vmem,
        out_shape=jax.ShapeDtypeStruct((rows, width), jnp.float32),
        compiler_params=params(24),
        cost_estimate=pl.CostEstimate(
            flops=2 * rows * width * pieces * block,
            bytes_accessed=2 * pieces * block * width + 4 * rows * width,
            transcendentals=0,
        ),
    )(left, near, far)


def pairs_of(size, bit):
    return [(i, i ^ bit) for i in range(size)]


def gather_mp(values, size):
    held = [value[None] for value in values]
    offsets = [0]
    bit = size // 2
    while bit:
        held = [jnp.concatenate([part, lax.ppermute(part, "mp", pairs_of(size, bit))], axis=0) for part in held]
        offsets = offsets + [offset ^ bit for offset in offsets]
        bit //= 2
    return held, offsets


def scatter_mp(value, size, index):
    width = value.shape[1] // size
    parts = [value[:, i * width : (i + 1) * width] for i in range(size)]
    bit = 1
    while bit < size:
        high = (index & bit) != 0
        keep = [jnp.where(high, parts[i + 1], parts[i]) for i in range(0, len(parts), 2)]
        sent = [jnp.where(high, parts[i], parts[i + 1]) for i in range(0, len(parts), 2)]
        got = lax.ppermute(jnp.concatenate(sent, axis=1), "mp", pairs_of(size, bit))
        parts = [part + got[:, i * width : (i + 1) * width] for i, part in enumerate(keep)]
        bit *= 2
    return parts[0]


def shards(tokens, cotangent, path_weights, outer_weights, momentum, assignment, owners):
    paths = lax.axis_size("path")
    ranks = lax.axis_size("mp")
    line = paths // FOLD
    me = lax.axis_index("path")
    rank = lax.axis_index("mp")
    z, side = me // FOLD, me % FOLD
    levels, units, width = path_weights.shape[1:]
    modules, block = outer_weights.shape[2], outer_weights.shape[4]
    scale_d = width ** (-0.5)
    scale_f = (units * ranks) ** (-0.5)

    (inputs, upstream), offsets = gather_mp([tokens, cotangent], ranks)
    spots = jnp.asarray([offsets.index(i) for i in range(ranks)], jnp.int32)
    rank_ids = jnp.arange(ranks, dtype=jnp.int32)
    order = jnp.sum(jnp.where((rank_ids ^ rank)[:, None] == rank_ids[None, :], spots[None, :], 0), axis=1)

    module_ids = jnp.arange(modules, dtype=jnp.int32)
    path_ids = jnp.arange(paths, dtype=jnp.int32)
    mine = lax.dynamic_index_in_dim(assignment, me, 1, keepdims=False)
    theirs = lax.dynamic_index_in_dim(assignment, me ^ 1, 1, keepdims=False)
    at_all = jnp.stack([mine, theirs, jnp.full_like(mine, z)], axis=1)
    is_mine = mine[:, None] == module_ids[None, :]
    shares = jnp.sum((assignment[:, None, :] == module_ids[None, :, None]).astype(jnp.float32), axis=2)
    owner_rows = jnp.sum(jnp.where(is_mine[:, :, None], owners, 0), axis=1)
    apart = (owner_rows % FOLD) ^ side
    leaves = jnp.stack([apart, owner_rows // FOLD], axis=1)
    slot = apart * line + (z - owner_rows // FOLD + line) % line
    piece_at = jnp.sum(
        jnp.where(slot[:, None, :] == path_ids[None, :, None], path_ids[None, None, :], 0), axis=2
    )
    down_at = jnp.sum(
        jnp.where(piece_at[1][:, None] == path_ids[None, :], slot[2][None, :], 0), axis=1
    )
    gate_table = piece_at[0][None]
    hidden_table = jnp.stack([piece_at[1], down_at])

    across = pairs_of(paths, 1)

    def permute(value, pairs):
        return lax.ppermute(value, "path", pairs)

    def along(values, first, last):
        up = [(i, i + FOLD) for i in range(paths - FOLD) if first <= i // FOLD <= last]
        low = [(paths - 1 - i, paths - 1 - j) for i, j in up]
        return [permute(values[0], up), permute(values[1], low)]

    half = width // STREAMS
    chunk = width // ranks
    narrow = chunk // STREAMS

    def columns(level, s):
        if level == 2:
            return (lambda t: t * STREAMS + s), ranks, narrow
        tile = min(chunk, half)
        return (lambda t: s * (half // tile) + t), half // tile, tile

    gate, upper, hidden = front(
        open_kernel, scale_d, order, inputs, path_weights, (0, 1), (), (jnp.float32, jnp.float32, jnp.bfloat16)
    )
    pre_gate, pre_up = front(
        close_kernel, scale_f, order, upstream, path_weights, (2,), (gate, upper), (jnp.bfloat16, jnp.bfloat16)
    )
    sources = ((pre_gate, inputs, scale_d), (pre_up, inputs, scale_d), (hidden, upstream, scale_f))

    flow = [[] for _ in range(STREAMS)]
    first = [[] for _ in range(STREAMS)]
    waiting = [None] * STREAMS
    near = [[None] * STREAMS for _ in range(levels)]
    far = [[None] * STREAMS for _ in range(levels)]
    whole = None
    hidden_new = gate_new = None

    def give(level, s):
        near[level][s], leaving = deliver(at_all[level], *waiting[s], [hidden_new] if level == 2 else [])
        far[level][s] = permute(leaving, across)

    outs = []
    for level in range(levels + 1):
        own, got = [None] * STREAMS, [None] * STREAMS
        if level < levels:
            left, right, scale = sources[level]
            for s in range(STREAMS):
                own[s], send = finals(
                    leaves[level], order, left, right, path_weights, level, columns(level, s), scale, line, block, first[s]
                )
                got[s] = permute(send, across)
        for step in range(1, line):
            for s in range(STREAMS):
                if level < levels:
                    value = running(at_all[level], own[s], got[s], flow[s], modules, step)
                    flow[s] = along(value, 0, step - 1 if level == 0 else line)
                elif step < line - 1:
                    flow[s] = along(flow[s], step, line)
                if step == 1:
                    first[s] = flow[s][:1]
                if waiting[s] is not None:
                    if step < line - 1:
                        waiting[s][1].append(flow[s][0])
                        waiting[s][2].append(flow[s][1])
                    if step == max(line - 2, 1):
                        give(level - 1, s)
        if level < levels:
            for s in range(STREAMS):
                after = [near[level - 1][s]] if level else []
                if level == 2:
                    after.append(gate_new)
                fresh, whole = update(
                    at_all[level], shares[level], own[s], got[s], flow[s], outer_weights, momentum, whole, level,
                    columns(level, s), after,
                )
                flow[s] = along((fresh, fresh), 0, line)
                waiting[s] = (fresh, [flow[s][0]], [flow[s][1]])
        if level == 1:
            gate_new = forward(
                gate_kernel, order, gate_table, inputs, (), near[0] + far[0], jnp.float32, scale_d, line, block
            )
        if level == 2:
            hidden_new = forward(
                hidden_kernel, order, hidden_table, inputs, (gate_new,), near[1] + far[1], jnp.bfloat16, scale_d,
                line, block,
            )
        if level == 3:
            for s in range(STREAMS):
                outs.append(scatter_mp(down(hidden_new, near[2][s], far[2][s], scale_f), ranks, rank))

    outputs = jnp.concatenate(outs, axis=1).astype(jnp.bfloat16)
    return outputs, whole


def solution(mesh):
    return jax.shard_map(
        shards,
        mesh=mesh,
        in_specs=(
            P("path", "mp"),
            P("path", "mp"),
            P("path", None, "mp", None),
            P("path", None, None, "mp", None, None),
            P("path", None, None, "mp", None, None),
            P(),
            P(),
        ),
        out_specs=(P("path", "mp"), P("path", None, None, "mp", None, None)),
        check_vma=False,
    )
```

```python
import functools

import jax
import jax.numpy as jnp
from jax import lax
from jax.experimental import pallas as pl
from jax.experimental.pallas import tpu as pltpu
from jax.sharding import PartitionSpec as P

mu_outer = 0.9
eta_outer = 0.7
lr_inner = 2.0

STREAMS = 2
BRIEF = pl.CostEstimate(flops=1, bytes_accessed=1, transcendentals=0)
FOLD = 2


def contract(left, right, left_dim, right_dim):
    return lax.dot_general(
        left, right, (((left_dim,), (right_dim,)), ((), ())), preferred_element_type=jnp.float32
    )


def params(mib):
    return pltpu.CompilerParams(vmem_limit_bytes=mib * 2**20)


def spread(position, left, right_ref, chunks):
    size = left.shape[1] // chunks
    total = None
    for j in range(chunks):
        value = contract(left[:, j * size : (j + 1) * size], right_ref[position(j)], 1, 1)
        total = value if total is None else total + value
    return total


def open_kernel(scale, chunks, order_ref, x_ref, gate_w_ref, up_w_ref, gate_ref, up_ref, hidden_ref):
    position = lambda j: order_ref[j]
    gate = spread(position, gate_w_ref[0, 0], x_ref, chunks) * scale
    upper = spread(position, up_w_ref[0, 0], x_ref, chunks) * scale
    gate_ref[...] = gate
    up_ref[...] = upper
    hidden_ref[...] = (gate * jax.nn.sigmoid(gate) * upper).astype(jnp.bfloat16)


def close_kernel(scale, chunks, order_ref, c_ref, weight_ref, gate_ref, up_ref, pre_gate_ref, pre_up_ref):
    grad = spread(lambda j: order_ref[j], weight_ref[0, 0], c_ref, chunks) * scale
    gate, upper = gate_ref[...], up_ref[...]
    sig = jax.nn.sigmoid(gate)
    act = gate * sig
    pre_gate_ref[...] = (grad * upper * sig * (1.0 + gate * (1.0 - sig))).astype(jnp.bfloat16)
    pre_up_ref[...] = (grad * act).astype(jnp.bfloat16)


def front(kernel, scale, order, right, weights, picked, extra, dtypes):
    chunks, rows, size = right.shape
    units, width = weights.shape[2:]
    tile = min(256, units)
    thin = pl.BlockSpec((tile, rows), lambda i, order: (i, 0))
    return pl.pallas_call(
        functools.partial(kernel, scale, chunks),
        grid_spec=pltpu.PrefetchScalarGridSpec(
            num_scalar_prefetch=1,
            grid=(units // tile,),
            in_specs=[pl.BlockSpec((chunks, rows, size), lambda i, order: (0, 0, 0))]
            + [
                pl.BlockSpec((1, 1, tile, width), lambda i, order, level=level: (0, level, i, 0))
                for level in picked
            ]
            + [thin] * len(extra),
            out_specs=[thin] * len(dtypes),
        ),
        out_shape=[jax.ShapeDtypeStruct((units, rows), dtype) for dtype in dtypes],
        compiler_params=params(16),
        cost_estimate=BRIEF,
    )(order, right, *[weights] * len(picked), *extra)


def finals_kernel(scale, block, pieces, split, table_ref, left_ref, right_ref, weight_ref, *refs):
    own_ref, send_refs = refs[0], refs[1:]
    line = own_ref.shape[0]
    grad = contract(left_ref[...], right_ref[0], 1, 0) * (lr_inner * scale)
    for q in range(pieces):
        rows = slice(q * block, (q + 1) * block)
        final = weight_ref[0, 0, rows, :].astype(jnp.float32) - grad[rows]
        spot = table_ref[1, q]
        leaves = table_ref[0, q] != 0
        outer = (spot == 0) | (spot == line - 1)

        @pl.when(jnp.logical_not(leaves))
        def _():
            own_ref[spot] = final

        if split:

            @pl.when(leaves & outer)
            def _():
                send_refs[0][jnp.where(spot == 0, 0, 1)] = final.astype(jnp.bfloat16)

            @pl.when(leaves & jnp.logical_not(outer))
            def _():
                send_refs[1][jnp.clip(spot - 1, 0, line - 3)] = final.astype(jnp.bfloat16)

        else:

            @pl.when(leaves)
            def _():
                send_refs[0][spot] = final.astype(jnp.bfloat16)


def finals(table, order, left, right, weights, level, columns, scale, line, block, split, after):
    start, tiles, tile = columns
    units, rows = left.shape
    per = right.shape[2] // tile
    width = tiles * tile
    counts = [line] + ([2, line - 2] if split else [line])

    def kernel(table_ref, order_ref, left_ref, right_ref, weight_ref, *refs):
        outs = refs[len(after) :]
        finals_kernel(scale, block, units // block, split, table_ref, left_ref, right_ref, weight_ref, *outs)

    return pl.pallas_call(
        kernel,
        grid_spec=pltpu.PrefetchScalarGridSpec(
            num_scalar_prefetch=2,
            grid=(tiles,),
            in_specs=[
                pl.BlockSpec((units, rows), lambda t, table, order: (0, 0)),
                pl.BlockSpec(
                    (1, rows, tile), lambda t, table, order: (order[start(t) // per], 0, start(t) % per)
                ),
                pl.BlockSpec((1, 1, units, tile), lambda t, table, order: (0, level, 0, start(t))),
            ]
            + [pl.BlockSpec(memory_space=pl.ANY)] * len(after),
            out_specs=[pl.BlockSpec((n, block, tile), lambda t, table, order: (0, 0, t)) for n in counts],
        ),
        out_shape=[
            jax.ShapeDtypeStruct((n, block, width), jnp.bfloat16 if i else jnp.float32)
            for i, n in enumerate(counts)
        ],
        compiler_params=params(16),
        cost_estimate=BRIEF,
    )(table, order, left, right, weights, *after)


def places(line, step):
    ups = lambda at: jnp.clip(line - step + at[2], 0, line - 1)
    downs = lambda at: jnp.clip(at[2] - line + step, 0, line - 1)
    return ups, downs


def running_kernel(line, step, flows, at_ref, *refs):
    own_refs, got_refs, flow_refs, out_refs = refs[:2], refs[2:4], refs[4 : 4 + flows], refs[-2:]
    modules = out_refs[0].shape[0]
    z = at_ref[2]
    lives = (z < step, z >= line - step)
    for way in range(2):
        for m in range(modules):
            total = jnp.where(lives[way] & (at_ref[0] == m), own_refs[way][0], 0.0)
            total = total + jnp.where(
                lives[way] & (at_ref[1] == m), got_refs[way][0].astype(jnp.float32), 0.0
            )
            if flow_refs:
                total = total + flow_refs[way][m].astype(jnp.float32)
            out_refs[way][m] = total.astype(jnp.bfloat16)


def running(at, own, got, flow, modules, step, outer, after):
    line, block, width = own.shape
    tile = min(512, width)
    both = places(line, step)
    one = lambda spot: pl.BlockSpec((1, block, tile), lambda t, at: (spot(at), 0, t))
    ends = (lambda at: 1, lambda at: 0)
    wide = pl.BlockSpec((modules, block, tile), lambda t, at: (0, 0, t))
    return pl.pallas_call(
        functools.partial(running_kernel, line, step, len(flow)),
        grid_spec=pltpu.PrefetchScalarGridSpec(
            num_scalar_prefetch=1,
            grid=(width // tile,),
            in_specs=[one(spot) for spot in both]
            + [one(spot) for spot in (ends if outer else both)]
            + [wide] * len(flow)
            + [pl.BlockSpec(memory_space=pl.ANY)] * len(after),
            out_specs=[wide, wide],
        ),
        out_shape=[jax.ShapeDtypeStruct((modules, block, width), jnp.bfloat16)] * 2,
        compiler_params=params(12),
        cost_estimate=BRIEF,
    )(at, own, own, got, got, *flow, *after)


def update_kernel(count, at_ref, share_ref, own_ref, got_ref, up_ref, low_ref, stored_ref, old_ref, *refs):
    fresh_ref, whole_ref = refs[-2:]
    for m in range(count):
        total = jnp.where(at_ref[0] == m, own_ref[0], 0.0)
        total = total + jnp.where(at_ref[1] == m, got_ref[0].astype(jnp.float32), 0.0)
        total = total + up_ref[m].astype(jnp.float32) + low_ref[m].astype(jnp.float32)
        stored = stored_ref[0, 0, m, 0]
        delta = stored - total / share_ref[m]
        velocity = mu_outer * old_ref[0, 0, m, 0].astype(jnp.float32) + delta
        fresh = (stored - eta_outer * (delta + mu_outer * velocity)).astype(jnp.bfloat16)
        fresh_ref[m] = fresh
        whole_ref[0, 0, m, 0] = fresh


def update(at, share, own, got, flow, outer_weights, momentum, whole, level, columns, after):
    start, tiles, tile = columns
    modules, block = outer_weights.shape[2], outer_weights.shape[4]
    one = pl.BlockSpec((1, block, tile), lambda t, at: (at[2], 0, t))
    wide = pl.BlockSpec((modules, block, tile), lambda t, at: (0, 0, t))
    state = pl.BlockSpec((1, 1, modules, 1, block, tile), lambda t, at: (0, level, 0, 0, 0, start(t)))
    extra = ([] if whole is None else [whole]) + after
    return pl.pallas_call(
        functools.partial(update_kernel, modules),
        grid_spec=pltpu.PrefetchScalarGridSpec(
            num_scalar_prefetch=1,
            grid=(tiles,),
            in_specs=[pl.BlockSpec(memory_space=pltpu.SMEM), one, one, wide, wide, state, state]
            + [pl.BlockSpec(memory_space=pl.ANY)] * len(extra),
            out_specs=[wide, state],
        ),
        out_shape=[
            jax.ShapeDtypeStruct((modules, block, tiles * tile), jnp.bfloat16),
            jax.ShapeDtypeStruct(outer_weights.shape, jnp.bfloat16),
        ],
        input_output_aliases={} if whole is None else {8: 1},
        compiler_params=params(16),
        cost_estimate=BRIEF,
    )(at, share, own, got, *flow, outer_weights, momentum, *extra)


def deliver_kernel(line, rings, at_ref, fresh_ref, *refs):
    ups, lows = refs[: len(rings)], refs[len(rings) : 2 * len(rings)]
    near_ref, far_ref, sems = refs[-3:]
    z = at_ref[2]
    for side, out_ref in enumerate((near_ref, far_ref)):
        module = at_ref[side]

        def copy(source, i, side=side, out_ref=out_ref, module=module):
            return pltpu.make_async_copy(source.at[module], out_ref.at[i], sems.at[side, i])

        for i, r in enumerate(rings):
            if r == 0:
                copy(fresh_ref, i).start()
                continue

            @pl.when(z >= r)
            def _():
                copy(ups[i], i).start()

            @pl.when(z < r)
            def _():
                copy(lows[i], i).start()

    for side, out_ref in enumerate((near_ref, far_ref)):
        for i in range(len(rings)):
            pltpu.make_async_copy(fresh_ref.at[0], out_ref.at[i], sems.at[side, i]).wait()


def deliver(at, fresh, ups, lows, line, rings, after):
    shape = jax.ShapeDtypeStruct((len(rings),) + fresh.shape[1:], fresh.dtype)
    anywhere = pl.BlockSpec(memory_space=pl.ANY)
    ups = [ups[r - 1] if r else fresh for r in rings]
    lows = [lows[line - 1 - r] if r else fresh for r in rings]
    return pl.pallas_call(
        functools.partial(deliver_kernel, line, rings),
        in_specs=[pl.BlockSpec(memory_space=pltpu.SMEM)] + [anywhere] * (2 * len(rings) + 1 + len(after)),
        out_specs=[pl.BlockSpec(memory_space=pltpu.VMEM)] * 2,
        out_shape=[shape, shape],
        scratch_shapes=[pltpu.SemaphoreType.DMA((2, len(rings)))],
        compiler_params=params(12),
        cost_estimate=BRIEF,
    )(at, fresh, *ups, *lows, *after)


def product(order_ref, x_ref, parts):
    total = None
    size = x_ref.shape[2]
    at = 0
    for part in parts:
        for i in range(part.shape[2] // size):
            left = part[:, :, i * size : (i + 1) * size].reshape(-1, size)
            value = contract(left, x_ref[order_ref[at]], 1, 1)
            total = value if total is None else total + value
            at += 1
    return total


def gate_kernel(scale, block, line, order_ref, table_ref, x_ref, *refs):
    out_ref = refs[-1]
    count = (len(refs) - 1) // 2
    for side, parts in enumerate((refs[:count], refs[count:-1])):
        value = product(order_ref, x_ref, parts) * scale
        for r in range(line):
            out_ref[table_ref[0, side * line + r]] = value[r * block : (r + 1) * block]


def hidden_kernel(scale, block, line, order_ref, table_ref, x_ref, gate_ref, *refs):
    out_ref = refs[-1]
    count = (len(refs) - 1) // 2
    for side, parts in enumerate((refs[:count], refs[count:-1])):
        value = product(order_ref, x_ref, parts) * scale
        for r in range(line):
            gate = gate_ref[table_ref[0, side * line + r]]
            upper = value[r * block : (r + 1) * block]
            hidden = gate * jax.nn.sigmoid(gate) * upper
            out_ref[table_ref[1, side * line + r]] = hidden.astype(jnp.bfloat16)


def forward(kernel, order, table, inputs, extra, parts, dtype, scale, line, block):
    chunks, rows, size = inputs.shape
    pieces = 2 * line
    smem = pl.BlockSpec(memory_space=pltpu.SMEM)
    vmem = pl.BlockSpec(memory_space=pltpu.VMEM)
    return pl.pallas_call(
        functools.partial(kernel, scale, block, line),
        in_specs=[smem, smem] + [vmem] * (1 + len(extra) + len(parts)),
        out_specs=vmem,
        out_shape=jax.ShapeDtypeStruct((pieces, block, rows), dtype),
        compiler_params=params(32),
        cost_estimate=BRIEF,
    )(order, table, inputs, *extra, *parts)


def down_kernel(scale, ranks, high_ref, left_ref, *refs):
    parts, keep_ref, send_ref = refs[:-2], refs[-2], refs[-1]
    rows = left_ref.shape[2]
    total = None
    at = 0
    for part in parts:
        count, block, width = part.shape
        left = left_ref[at : at + count].reshape(count * block, rows)
        value = contract(left, part[...].reshape(count * block, width), 0, 0)
        total = value if total is None else total + value
        at += count
    total = total * scale
    size = width // ranks
    high = high_ref[0] != 0
    for i in range(ranks // 2):
        low_part = total[:, 2 * i * size : (2 * i + 1) * size]
        high_part = total[:, (2 * i + 1) * size : (2 * i + 2) * size]
        spot = slice(i * size, (i + 1) * size)
        keep_ref[:, spot] = jnp.where(high, high_part, low_part)
        send_ref[:, spot] = jnp.where(high, low_part, high_part).astype(jnp.bfloat16)


def down(high, left, parts, ranks, scale):
    pieces, block, rows = left.shape
    width = parts[0].shape[2]
    vmem = pl.BlockSpec(memory_space=pltpu.VMEM)
    return pl.pallas_call(
        functools.partial(down_kernel, scale, ranks),
        in_specs=[pl.BlockSpec(memory_space=pltpu.SMEM)] + [vmem] * (1 + len(parts)),
        out_specs=[vmem] * 2,
        out_shape=[
            jax.ShapeDtypeStruct((rows, width // 2), jnp.float32),
            jax.ShapeDtypeStruct((rows, width // 2), jnp.bfloat16),
        ],
        compiler_params=params(24),
        cost_estimate=BRIEF,
    )(high, left, *parts)


def pairs_of(size, bit):
    return [(i, i ^ bit) for i in range(size)]


def gather_mp(values, size):
    held = [[value[None]] for value in values]
    offsets = [0]
    bit = size // 2
    while bit:
        held = [parts + [lax.ppermute(part, "mp", pairs_of(size, bit)) for part in parts] for parts in held]
        offsets = offsets + [offset ^ bit for offset in offsets]
        bit //= 2
    return [jnp.concatenate(parts, axis=0) for parts in held], offsets


def scatter_mp(keep, send, size, index):
    width = 2 * keep.shape[1] // size
    value = keep + lax.ppermute(send, "mp", pairs_of(size, 1)).astype(jnp.float32)
    bit = 2
    while bit < size:
        parts = [value[:, at : at + width] for at in range(0, value.shape[1], width)]
        high = (index & bit) != 0
        keep = [jnp.where(high, parts[i + 1], parts[i]) for i in range(0, len(parts), 2)]
        send = [jnp.where(high, parts[i], parts[i + 1]) for i in range(0, len(parts), 2)]
        got = lax.ppermute(jnp.concatenate(send, axis=1).astype(jnp.bfloat16), "mp", pairs_of(size, bit))
        value = jnp.concatenate(keep, axis=1) + got.astype(jnp.float32)
        bit *= 2
    return value


def shards(tokens, cotangent, path_weights, outer_weights, momentum, assignment, owners):
    paths = lax.axis_size("path")
    ranks = lax.axis_size("mp")
    line = paths // FOLD
    me = lax.axis_index("path")
    rank = lax.axis_index("mp")
    z, side = me // FOLD, me % FOLD
    levels, units, width = path_weights.shape[1:]
    modules, block = outer_weights.shape[2], outer_weights.shape[4]
    scale_d = width ** (-0.5)
    scale_f = (units * ranks) ** (-0.5)

    (inputs, upstream), offsets = gather_mp([tokens, cotangent], ranks)
    spots = jnp.asarray([offsets.index(i) for i in range(ranks)], jnp.int32)
    rank_ids = jnp.arange(ranks, dtype=jnp.int32)
    order = jnp.sum(jnp.where((rank_ids ^ rank)[:, None] == rank_ids[None, :], spots[None, :], 0), axis=1)

    module_ids = jnp.arange(modules, dtype=jnp.int32)
    path_ids = jnp.arange(paths, dtype=jnp.int32)
    mine = lax.dynamic_index_in_dim(assignment, me, 1, keepdims=False)
    theirs = lax.dynamic_index_in_dim(assignment, me ^ 1, 1, keepdims=False)
    at_all = jnp.stack([mine, theirs, jnp.full_like(mine, z)], axis=1)
    is_mine = mine[:, None] == module_ids[None, :]
    shares = jnp.sum((assignment[:, None, :] == module_ids[None, :, None]).astype(jnp.float32), axis=2)
    owner_rows = jnp.sum(jnp.where(is_mine[:, :, None], owners, 0), axis=1)
    apart = (owner_rows % FOLD) ^ side
    leaves = jnp.stack([apart, owner_rows // FOLD], axis=1)
    slot = apart * line + (z - owner_rows // FOLD + line) % line
    piece_at = jnp.sum(
        jnp.where(slot[:, None, :] == path_ids[None, :, None], path_ids[None, None, :], 0), axis=2
    )
    down_at = jnp.sum(
        jnp.where(piece_at[1][:, None] == path_ids[None, :], slot[2][None, :], 0), axis=1
    )
    across = pairs_of(paths, 1)

    def permute(value, pairs):
        return lax.ppermute(value, "path", pairs)

    def along(values, first, last):
        up = [(i, i + FOLD) for i in range(paths - FOLD) if first <= i // FOLD <= last]
        low = [(paths - 1 - i, paths - 1 - j) for i, j in up]
        return [permute(values[0], up), permute(values[1], low)]

    half = width // STREAMS
    chunk = width // ranks
    narrow = chunk // STREAMS

    def columns(level, s):
        if level == 2:
            return (lambda t: t * STREAMS + s), ranks, narrow
        tile = min(chunk, half)
        return (lambda t: s * (half // tile) + t), half // tile, tile

    gate, upper, hidden = front(
        open_kernel, scale_d, order, inputs, path_weights, (0, 1), (), (jnp.float32, jnp.float32, jnp.bfloat16)
    )
    pre_gate, pre_up = front(
        close_kernel, scale_f, order, upstream, path_weights, (2,), (gate, upper), (jnp.bfloat16, jnp.bfloat16)
    )
    sources = ((pre_gate, inputs, scale_d), (pre_up, inputs, scale_d), (hidden, upstream, scale_f))

    late = [r for r in range(line) if max(r - 1, line - 1 - r) == line - 2 and r]
    soon = [r for r in range(line) if r not in late]
    parts_of = [(side, r) for rings in (soon, late) for side in range(FOLD) for r in rings]
    turn = jnp.asarray([parts_of.index((e // line, e % line)) for e in range(paths)], jnp.int32)
    down_at = jnp.sum(jnp.where(down_at[:, None] == path_ids[None, :], turn[None, :], 0), axis=1)
    gate_table = piece_at[0][None]
    hidden_table = jnp.stack([piece_at[1], down_at])
    high = (rank & 1)[None]

    flow = [[] for _ in range(STREAMS)]
    first = [[] for _ in range(STREAMS)]
    waiting = [None] * STREAMS
    near = [[[] for _ in range(STREAMS)] for _ in range(levels)]
    far = [[[] for _ in range(STREAMS)] for _ in range(levels)]
    whole = None
    hidden_new = gate_new = None

    def give(level, s, rings, after):
        fresh, ups, lows = waiting[s]
        held, leaving = deliver(at_all[level], fresh, ups, lows, line, rings, after)
        near[level][s].append(held)
        far[level][s].append(permute(leaving, across))

    def ring_parts(level):
        return [part for half in (near, far) for s in range(STREAMS) for part in half[level][s]]

    outs = []
    for level in range(levels + 1):
        own, got, ends = [None] * STREAMS, [None] * STREAMS, [None] * STREAMS
        split = level == 0 and line > 2
        if level < levels:
            left, right, scale = sources[level]
            for s in range(STREAMS):
                own[s], *sent = finals(
                    leaves[level], order, left, right, path_weights, level, columns(level, s), scale, line, block,
                    split, first[s],
                )
                if split:
                    ends[s] = permute(sent[0], across)
                    middle = permute(sent[1], across)
                    got[s] = jnp.concatenate([ends[s][:1], middle, ends[s][1:]], axis=0)
                else:
                    got[s] = permute(sent[0], across)
        for step in range(1, line):
            for s in range(STREAMS):
                if level < levels:
                    outer = split and step == 1
                    after = near[level - 1][s] if level and step == line - 1 else []
                    value = running(
                        at_all[level], own[s], ends[s] if outer else got[s], flow[s], modules, step, outer, after
                    )
                    flow[s] = along(value, 0, step - 1 if level == 0 else line)
                elif step < line - 1:
                    flow[s] = along(flow[s], step, line)
                if step == 1:
                    first[s] = flow[s][:1]
                if waiting[s] is not None:
                    if step < line - 1:
                        waiting[s][1].append(flow[s][0])
                        waiting[s][2].append(flow[s][1])
                    if level < levels and step == max(line - 2, 1):
                        give(level - 1, s, tuple(range(line)), [])
                    if level == levels:
                        if step == max(line - 3, 1):
                            give(level - 1, s, tuple(soon), [hidden_new])
                        if step == max(line - 2, 1):
                            give(level - 1, s, tuple(late), [])
        if level < levels:
            for s in range(STREAMS):
                after = [gate_new] if level == 2 else []
                fresh, whole = update(
                    at_all[level], shares[level], own[s], got[s], flow[s], outer_weights, momentum, whole, level,
                    columns(level, s), after,
                )
                flow[s] = along((fresh, fresh), 0, line)
                waiting[s] = (fresh, [flow[s][0]], [flow[s][1]])
        if level == 1:
            gate_new = forward(
                gate_kernel, order, gate_table, inputs, (), ring_parts(0), jnp.float32, scale_d, line, block
            )
        if level == 2:
            hidden_new = forward(
                hidden_kernel, order, hidden_table, inputs, (gate_new,), ring_parts(1), jnp.bfloat16, scale_d,
                line, block,
            )
        if level == 3:
            for s in range(STREAMS):
                parts = [part for pair in zip(near[2][s], far[2][s]) for part in pair]
                keep, send = down(high, hidden_new, parts, ranks, scale_f)
                outs.append(scatter_mp(keep, send, ranks, rank))

    outputs = jnp.concatenate(outs, axis=1).astype(jnp.bfloat16)
    return outputs, whole


def solution(mesh):
    return jax.shard_map(
        shards,
        mesh=mesh,
        in_specs=(
            P("path", "mp"),
            P("path", "mp"),
            P("path", None, "mp", None),
            P("path", None, None, "mp", None, None),
            P("path", None, None, "mp", None, None),
            P(),
            P(),
        ),
        out_specs=(P("path", "mp"), P("path", None, None, "mp", None, None)),
        check_vma=False,
    )
```

```python
import functools

import jax
import jax.numpy as jnp
from jax import lax
from jax.experimental import pallas as pl
from jax.experimental.pallas import tpu as pltpu
from jax.sharding import PartitionSpec as P

mu_outer = 0.9
eta_outer = 0.7
lr_inner = 2.0

STREAMS = 2
BRIEF = pl.CostEstimate(flops=1, bytes_accessed=1, transcendentals=0)
FOLD = 2


def contract(left, right, left_dim, right_dim):
    return lax.dot_general(
        left, right, (((left_dim,), (right_dim,)), ((), ())), preferred_element_type=jnp.float32
    )


def params(mib):
    return pltpu.CompilerParams(vmem_limit_bytes=mib * 2**20)


def spread(position, left, right_ref, chunks):
    size = left.shape[1] // chunks
    total = None
    for j in range(chunks):
        value = contract(left[:, j * size : (j + 1) * size], right_ref[position(j)], 1, 1)
        total = value if total is None else total + value
    return total


def open_kernel(scale, chunks, order_ref, x_ref, gate_w_ref, up_w_ref, gate_ref, up_ref, hidden_ref):
    position = lambda j: order_ref[j]
    gate = spread(position, gate_w_ref[0, 0], x_ref, chunks) * scale
    upper = spread(position, up_w_ref[0, 0], x_ref, chunks) * scale
    gate_ref[...] = gate
    up_ref[...] = upper
    hidden_ref[...] = (gate * jax.nn.sigmoid(gate) * upper).astype(jnp.bfloat16)


def close_kernel(scale, chunks, order_ref, c_ref, weight_ref, gate_ref, up_ref, pre_gate_ref, pre_up_ref):
    grad = spread(lambda j: order_ref[j], weight_ref[0, 0], c_ref, chunks) * scale
    gate, upper = gate_ref[...], up_ref[...]
    sig = jax.nn.sigmoid(gate)
    act = gate * sig
    pre_gate_ref[...] = (grad * upper * sig * (1.0 + gate * (1.0 - sig))).astype(jnp.bfloat16)
    pre_up_ref[...] = (grad * act).astype(jnp.bfloat16)


def front(kernel, scale, order, right, weights, picked, extra, dtypes):
    chunks, rows, size = right.shape
    units, width = weights.shape[2:]
    tile = min(256, units)
    thin = pl.BlockSpec((tile, rows), lambda i, order: (i, 0))
    return pl.pallas_call(
        functools.partial(kernel, scale, chunks),
        grid_spec=pltpu.PrefetchScalarGridSpec(
            num_scalar_prefetch=1,
            grid=(units // tile,),
            in_specs=[pl.BlockSpec((chunks, rows, size), lambda i, order: (0, 0, 0))]
            + [
                pl.BlockSpec((1, 1, tile, width), lambda i, order, level=level: (0, level, i, 0))
                for level in picked
            ]
            + [thin] * len(extra),
            out_specs=[thin] * len(dtypes),
        ),
        out_shape=[jax.ShapeDtypeStruct((units, rows), dtype) for dtype in dtypes],
        compiler_params=params(16),
        cost_estimate=BRIEF,
    )(order, right, *[weights] * len(picked), *extra)


def tie(value, after):
    anywhere = pl.BlockSpec(memory_space=pl.ANY)
    return pl.pallas_call(
        lambda *refs: None,
        in_specs=[anywhere] * (1 + len(after)),
        out_specs=anywhere,
        out_shape=jax.ShapeDtypeStruct(value.shape, value.dtype),
        input_output_aliases={0: 0},
        compiler_params=params(1),
        cost_estimate=BRIEF,
    )(value, *after)


def finals_kernel(scale, block, pieces, split, table_ref, left_ref, right_ref, weight_ref, *refs):
    own_ref, send_refs = refs[0], refs[1:]
    line = own_ref.shape[0]
    grad = contract(left_ref[...], right_ref[0], 1, 0) * (lr_inner * scale)
    for q in range(pieces):
        rows = slice(q * block, (q + 1) * block)
        final = weight_ref[0, 0, rows, :].astype(jnp.float32) - grad[rows]
        spot = table_ref[1, q]
        leaves = table_ref[0, q] != 0
        outer = (spot == 0) | (spot == line - 1)

        @pl.when(jnp.logical_not(leaves))
        def _():
            own_ref[spot] = final

        if split:

            @pl.when(leaves & outer)
            def _():
                send_refs[0][jnp.where(spot == 0, 0, 1)] = final.astype(jnp.bfloat16)

            @pl.when(leaves & jnp.logical_not(outer))
            def _():
                send_refs[1][jnp.clip(spot - 1, 0, line - 3)] = final.astype(jnp.bfloat16)

        else:

            @pl.when(leaves)
            def _():
                send_refs[0][spot] = final.astype(jnp.bfloat16)


def finals(table, order, left, right, weights, level, columns, scale, line, block, split, after):
    start, tiles, tile = columns
    units, rows = left.shape
    per = right.shape[2] // tile
    width = tiles * tile
    counts = [line] + ([2, line - 2] if split else [line])

    def kernel(table_ref, order_ref, left_ref, right_ref, weight_ref, *refs):
        outs = refs[len(after) :]
        finals_kernel(scale, block, units // block, split, table_ref, left_ref, right_ref, weight_ref, *outs)

    return pl.pallas_call(
        kernel,
        grid_spec=pltpu.PrefetchScalarGridSpec(
            num_scalar_prefetch=2,
            grid=(tiles,),
            in_specs=[
                pl.BlockSpec((units, rows), lambda t, table, order: (0, 0)),
                pl.BlockSpec(
                    (1, rows, tile), lambda t, table, order: (order[start(t) // per], 0, start(t) % per)
                ),
                pl.BlockSpec((1, 1, units, tile), lambda t, table, order: (0, level, 0, start(t))),
            ]
            + [pl.BlockSpec(memory_space=pl.ANY)] * len(after),
            out_specs=[pl.BlockSpec((n, block, tile), lambda t, table, order: (0, 0, t)) for n in counts],
        ),
        out_shape=[
            jax.ShapeDtypeStruct((n, block, width), jnp.bfloat16 if i else jnp.float32)
            for i, n in enumerate(counts)
        ],
        compiler_params=params(16),
        cost_estimate=BRIEF,
    )(table, order, left, right, weights, *after)


def places(line, step):
    ups = lambda at: jnp.clip(line - step + at[2], 0, line - 1)
    downs = lambda at: jnp.clip(at[2] - line + step, 0, line - 1)
    return ups, downs


def running_kernel(line, step, flows, outs, at_ref, *refs):
    own_refs, got_refs, flow_refs, out_refs = refs[:2], refs[2:4], refs[4 : 4 + flows], refs[-outs:]
    modules = out_refs[0].shape[0]
    z = at_ref[2]
    lives = (z < step, z >= line - step)
    lower = 2 * z < line
    for m in range(modules):
        totals = []
        for way in range(2):
            total = jnp.where(lives[way] & (at_ref[0] == m), own_refs[way][0], 0.0)
            total = total + jnp.where(
                lives[way] & (at_ref[1] == m), got_refs[way][0].astype(jnp.float32), 0.0
            )
            if flows == 2:
                total = total + flow_refs[way][m].astype(jnp.float32)
            if flows == 1:
                mine = lower if way == 0 else jnp.logical_not(lower)
                total = total + jnp.where(mine, flow_refs[0][m].astype(jnp.float32), 0.0)
            totals.append(total)
        if outs == 1:
            totals = [jnp.where(lower, totals[0], totals[1])]
        for total, out_ref in zip(totals, out_refs):
            out_ref[m] = total.astype(jnp.bfloat16)


def running(at, own, got, flow, modules, step, outer, after):
    line, block, width = own.shape
    outs = 1 if not flow and line > 3 else 2
    tile = min(512, width)
    both = places(line, step)
    one = lambda spot: pl.BlockSpec((1, block, tile), lambda t, at: (spot(at), 0, t))
    ends = (lambda at: 1, lambda at: 0)
    wide = pl.BlockSpec((modules, block, tile), lambda t, at: (0, 0, t))
    return pl.pallas_call(
        functools.partial(running_kernel, line, step, len(flow), outs),
        grid_spec=pltpu.PrefetchScalarGridSpec(
            num_scalar_prefetch=1,
            grid=(width // tile,),
            in_specs=[one(spot) for spot in both]
            + [one(spot) for spot in (ends if outer else both)]
            + [wide] * len(flow)
            + [pl.BlockSpec(memory_space=pl.ANY)] * len(after),
            out_specs=[wide] * outs,
        ),
        out_shape=[jax.ShapeDtypeStruct((modules, block, width), jnp.bfloat16)] * outs,
        compiler_params=params(12),
        cost_estimate=BRIEF,
    )(at, own, own, got, got, *flow, *after)


def update_kernel(count, at_ref, share_ref, own_ref, got_ref, up_ref, low_ref, stored_ref, old_ref, *refs):
    fresh_ref, whole_ref = refs[-2:]
    for m in range(count):
        total = jnp.where(at_ref[0] == m, own_ref[0], 0.0)
        total = total + jnp.where(at_ref[1] == m, got_ref[0].astype(jnp.float32), 0.0)
        total = total + up_ref[m].astype(jnp.float32) + low_ref[m].astype(jnp.float32)
        stored = stored_ref[0, 0, m, 0]
        delta = stored - total / share_ref[m]
        velocity = mu_outer * old_ref[0, 0, m, 0].astype(jnp.float32) + delta
        fresh = (stored - eta_outer * (delta + mu_outer * velocity)).astype(jnp.bfloat16)
        fresh_ref[m] = fresh
        whole_ref[0, 0, m, 0] = fresh


def update(at, share, own, got, flow, outer_weights, momentum, whole, level, columns, after):
    start, tiles, tile = columns
    modules, block = outer_weights.shape[2], outer_weights.shape[4]
    one = pl.BlockSpec((1, block, tile), lambda t, at: (at[2], 0, t))
    wide = pl.BlockSpec((modules, block, tile), lambda t, at: (0, 0, t))
    state = pl.BlockSpec((1, 1, modules, 1, block, tile), lambda t, at: (0, level, 0, 0, 0, start(t)))
    extra = ([] if whole is None else [whole]) + after
    return pl.pallas_call(
        functools.partial(update_kernel, modules),
        grid_spec=pltpu.PrefetchScalarGridSpec(
            num_scalar_prefetch=1,
            grid=(tiles,),
            in_specs=[pl.BlockSpec(memory_space=pltpu.SMEM), one, one, wide, wide, state, state]
            + [pl.BlockSpec(memory_space=pl.ANY)] * len(extra),
            out_specs=[wide, state],
        ),
        out_shape=[
            jax.ShapeDtypeStruct((modules, block, tiles * tile), jnp.bfloat16),
            jax.ShapeDtypeStruct(outer_weights.shape, jnp.bfloat16),
        ],
        input_output_aliases={} if whole is None else {8: 1},
        compiler_params=params(16),
        cost_estimate=BRIEF,
    )(at, share, own, got, *flow, outer_weights, momentum, *extra)


def deliver_kernel(line, rings, at_ref, fresh_ref, *refs):
    ups, lows = refs[: len(rings)], refs[len(rings) : 2 * len(rings)]
    near_ref, far_ref, sems = refs[-3:]
    z = at_ref[2]
    for side, out_ref in enumerate((near_ref, far_ref)):
        module = at_ref[side]

        def copy(source, i, side=side, out_ref=out_ref, module=module):
            return pltpu.make_async_copy(source.at[module], out_ref.at[i], sems.at[side, i])

        for i, r in enumerate(rings):
            if r == 0:
                copy(fresh_ref, i).start()
                continue

            @pl.when(z >= r)
            def _():
                copy(ups[i], i).start()

            @pl.when(z < r)
            def _():
                copy(lows[i], i).start()

    for side, out_ref in enumerate((near_ref, far_ref)):
        for i in range(len(rings)):
            pltpu.make_async_copy(fresh_ref.at[0], out_ref.at[i], sems.at[side, i]).wait()


def deliver(at, fresh, ups, lows, line, rings, after):
    shape = jax.ShapeDtypeStruct((len(rings),) + fresh.shape[1:], fresh.dtype)
    anywhere = pl.BlockSpec(memory_space=pl.ANY)
    ups = [ups[r - 1] if r else fresh for r in rings]
    lows = [lows[line - 1 - r] if r else fresh for r in rings]
    return pl.pallas_call(
        functools.partial(deliver_kernel, line, rings),
        in_specs=[pl.BlockSpec(memory_space=pltpu.SMEM)] + [anywhere] * (2 * len(rings) + 1 + len(after)),
        out_specs=[pl.BlockSpec(memory_space=pltpu.VMEM)] * 2,
        out_shape=[shape, shape],
        scratch_shapes=[pltpu.SemaphoreType.DMA((2, len(rings)))],
        compiler_params=params(12),
        cost_estimate=BRIEF,
    )(at, fresh, *ups, *lows, *after)


def product(order_ref, x_ref, parts):
    total = None
    size = x_ref.shape[2]
    at = 0
    for part in parts:
        for i in range(part.shape[2] // size):
            left = part[:, :, i * size : (i + 1) * size].reshape(-1, size)
            value = contract(left, x_ref[order_ref[at]], 1, 1)
            total = value if total is None else total + value
            at += 1
    return total


def gate_kernel(scale, block, line, order_ref, table_ref, x_ref, *refs):
    out_ref = refs[-1]
    count = (len(refs) - 1) // 2
    for side, parts in enumerate((refs[:count], refs[count:-1])):
        value = product(order_ref, x_ref, parts) * scale
        for r in range(line):
            out_ref[table_ref[0, side * line + r]] = value[r * block : (r + 1) * block]


def hidden_kernel(scale, block, line, order_ref, table_ref, x_ref, gate_ref, *refs):
    out_ref = refs[-1]
    count = (len(refs) - 1) // 2
    for side, parts in enumerate((refs[:count], refs[count:-1])):
        value = product(order_ref, x_ref, parts) * scale
        for r in range(line):
            gate = gate_ref[table_ref[0, side * line + r]]
            upper = value[r * block : (r + 1) * block]
            hidden = gate * jax.nn.sigmoid(gate) * upper
            out_ref[table_ref[1, side * line + r]] = hidden.astype(jnp.bfloat16)


def forward(kernel, order, table, inputs, extra, parts, dtype, scale, line, block):
    chunks, rows, size = inputs.shape
    pieces = 2 * line
    smem = pl.BlockSpec(memory_space=pltpu.SMEM)
    vmem = pl.BlockSpec(memory_space=pltpu.VMEM)
    return pl.pallas_call(
        functools.partial(kernel, scale, block, line),
        in_specs=[smem, smem] + [vmem] * (1 + len(extra) + len(parts)),
        out_specs=vmem,
        out_shape=jax.ShapeDtypeStruct((pieces, block, rows), dtype),
        compiler_params=params(32),
        cost_estimate=BRIEF,
    )(order, table, inputs, *extra, *parts)


def down_kernel(scale, ranks, high_ref, left_ref, *refs):
    parts, keep_ref, send_ref = refs[:-2], refs[-2], refs[-1]
    rows = left_ref.shape[2]
    total = None
    at = 0
    for part in parts:
        count, block, width = part.shape
        left = left_ref[at : at + count].reshape(count * block, rows)
        value = contract(left, part[...].reshape(count * block, width), 0, 0)
        total = value if total is None else total + value
        at += count
    total = total * scale
    size = width // ranks
    high = high_ref[0] != 0
    for i in range(ranks // 2):
        low_part = total[:, 2 * i * size : (2 * i + 1) * size]
        high_part = total[:, (2 * i + 1) * size : (2 * i + 2) * size]
        spot = slice(i * size, (i + 1) * size)
        keep_ref[:, spot] = jnp.where(high, high_part, low_part)
        send_ref[:, spot] = jnp.where(high, low_part, high_part).astype(jnp.bfloat16)


def down(high, left, parts, ranks, scale):
    pieces, block, rows = left.shape
    width = parts[0].shape[2]
    vmem = pl.BlockSpec(memory_space=pltpu.VMEM)
    return pl.pallas_call(
        functools.partial(down_kernel, scale, ranks),
        in_specs=[pl.BlockSpec(memory_space=pltpu.SMEM)] + [vmem] * (1 + len(parts)),
        out_specs=[vmem] * 2,
        out_shape=[
            jax.ShapeDtypeStruct((rows, width // 2), jnp.float32),
            jax.ShapeDtypeStruct((rows, width // 2), jnp.bfloat16),
        ],
        compiler_params=params(24),
        cost_estimate=BRIEF,
    )(high, left, *parts)


def pairs_of(size, bit):
    return [(i, i ^ bit) for i in range(size)]


def gather_mp(values, size):
    held = [[value[None]] for value in values]
    offsets = [0]
    bit = size // 2
    while bit:
        held = [parts + [lax.ppermute(part, "mp", pairs_of(size, bit)) for part in parts] for parts in held]
        offsets = offsets + [offset ^ bit for offset in offsets]
        bit //= 2
    return held, offsets


def scatter_mp(keep, send, size, index):
    width = 2 * keep.shape[1] // size
    value = keep + lax.ppermute(send, "mp", pairs_of(size, 1)).astype(jnp.float32)
    bit = 2
    while bit < size:
        parts = [value[:, at : at + width] for at in range(0, value.shape[1], width)]
        high = (index & bit) != 0
        keep = [jnp.where(high, parts[i + 1], parts[i]) for i in range(0, len(parts), 2)]
        send = [jnp.where(high, parts[i], parts[i + 1]) for i in range(0, len(parts), 2)]
        got = lax.ppermute(jnp.concatenate(send, axis=1).astype(jnp.bfloat16), "mp", pairs_of(size, bit))
        value = jnp.concatenate(keep, axis=1) + got.astype(jnp.float32)
        bit *= 2
    return value


def shards(tokens, cotangent, path_weights, outer_weights, momentum, assignment, owners):
    paths = lax.axis_size("path")
    ranks = lax.axis_size("mp")
    line = paths // FOLD
    me = lax.axis_index("path")
    rank = lax.axis_index("mp")
    z, side = me // FOLD, me % FOLD
    levels, units, width = path_weights.shape[1:]
    modules, block = outer_weights.shape[2], outer_weights.shape[4]
    scale_d = width ** (-0.5)
    scale_f = (units * ranks) ** (-0.5)

    held, offsets = gather_mp([tokens, cotangent], ranks)
    inputs, upstream = (jnp.concatenate(parts, axis=0) for parts in held)
    spots = jnp.asarray([offsets.index(i) for i in range(ranks)], jnp.int32)
    rank_ids = jnp.arange(ranks, dtype=jnp.int32)
    order = jnp.sum(jnp.where((rank_ids ^ rank)[:, None] == rank_ids[None, :], spots[None, :], 0), axis=1)

    module_ids = jnp.arange(modules, dtype=jnp.int32)
    path_ids = jnp.arange(paths, dtype=jnp.int32)
    mine = lax.dynamic_index_in_dim(assignment, me, 1, keepdims=False)
    theirs = lax.dynamic_index_in_dim(assignment, me ^ 1, 1, keepdims=False)
    at_all = jnp.stack([mine, theirs, jnp.full_like(mine, z)], axis=1)
    is_mine = mine[:, None] == module_ids[None, :]
    shares = jnp.sum((assignment[:, None, :] == module_ids[None, :, None]).astype(jnp.float32), axis=2)
    owner_rows = jnp.sum(jnp.where(is_mine[:, :, None], owners, 0), axis=1)
    apart = (owner_rows % FOLD) ^ side
    leaves = jnp.stack([apart, owner_rows // FOLD], axis=1)
    slot = apart * line + (z - owner_rows // FOLD + line) % line
    piece_at = jnp.sum(
        jnp.where(slot[:, None, :] == path_ids[None, :, None], path_ids[None, None, :], 0), axis=2
    )
    down_at = jnp.sum(
        jnp.where(piece_at[1][:, None] == path_ids[None, :], slot[2][None, :], 0), axis=1
    )
    across = pairs_of(paths, 1)

    def permute(value, pairs):
        return lax.ppermute(value, "path", pairs)

    def along(values, first, last):
        up = [(i, i + FOLD) for i in range(paths - FOLD) if first <= i // FOLD <= last]
        low = [(paths - 1 - i, paths - 1 - j) for i, j in up]
        if len(values) == 1:
            return [permute(values[0], up + low)]
        return [permute(values[0], up), permute(values[1], low)]

    half = width // STREAMS
    chunk = width // ranks
    narrow = chunk // STREAMS

    def columns(level, s):
        if level == 2:
            return (lambda t: t * STREAMS + s), ranks, narrow
        tile = min(chunk, half)
        return (lambda t: s * (half // tile) + t), half // tile, tile

    gate, upper, hidden = front(
        open_kernel, scale_d, order, inputs, path_weights, (0, 1), (), (jnp.float32, jnp.float32, jnp.bfloat16)
    )
    pre_gate, pre_up = front(
        close_kernel, scale_f, order, upstream, path_weights, (2,), (gate, upper), (jnp.bfloat16, jnp.bfloat16)
    )
    sources = ((pre_gate, inputs, scale_d), (pre_up, inputs, scale_d), (hidden, upstream, scale_f))

    late = [r for r in range(line) if max(r - 1, line - 1 - r) == line - 2 and r]
    soon = [r for r in range(1, line) if r not in late]
    parts_of = [(side, r) for rings in ([0], soon, late) for side in range(FOLD) for r in rings]
    turn = jnp.asarray([parts_of.index((e // line, e % line)) for e in range(paths)], jnp.int32)
    down_at = jnp.sum(jnp.where(down_at[:, None] == path_ids[None, :], turn[None, :], 0), axis=1)
    gate_table = piece_at[0][None]
    hidden_table = jnp.stack([piece_at[1], down_at])
    high = (rank & 1)[None]

    flow = [[] for _ in range(STREAMS)]
    first = [[[] for _ in range(STREAMS)] for _ in range(levels)]
    waiting = [None] * STREAMS
    near = [[[] for _ in range(STREAMS)] for _ in range(levels)]
    far = [[[] for _ in range(STREAMS)] for _ in range(levels)]
    whole = None
    hidden_new = gate_new = None

    def give(level, s, rings, after):
        fresh, ups, lows = waiting[s]
        held, leaving = deliver(at_all[level], fresh, ups, lows, line, rings, after)
        near[level][s].append(held)
        far[level][s].append(permute(leaving, across))

    def ring_parts(level):
        return [part for half in (near, far) for s in range(STREAMS) for part in half[level][s]]

    own = [[None] * STREAMS for _ in range(levels)]
    got = [[None] * STREAMS for _ in range(levels)]
    ends = [None] * STREAMS

    def prepare(level):
        left, right, scale = sources[level]
        for s in range(STREAMS):
            own[level][s], *sent = finals(
                leaves[level], order, left, right, path_weights, level, columns(level, s), scale, line, block,
                level == 0 and line > 2, first[level][s],
            )
            if len(sent) > 1:
                ends[s] = permute(sent[0], across)
                middle = permute(sent[1], across)
                got[level][s] = jnp.concatenate([ends[s][:1], middle, ends[s][1:]], axis=0)
            else:
                got[level][s] = permute(sent[0], across)

    outs = []
    for level in range(levels + 1):
        if level == 0:
            prepare(0)
        if level == 1:
            prepare(1)
            prepare(2)
        if level == 2:
            gate_new = forward(
                gate_kernel, order, gate_table, inputs, (), ring_parts(0), jnp.float32, scale_d, line, block
            )
        for step in range(1, line):
            for s in range(STREAMS):
                if level < levels:
                    outer = level == 0 and line > 2 and step == 1
                    after = near[level - 1][s] if level and step == line - 1 else []
                    if level == 1 and step == line - 1:
                        after = after + [got[2][s]]
                    if level == 2 and step == line - 2 and s == 0:
                        after = after + [gate_new]
                    value = running(
                        at_all[level], own[level][s], ends[s] if outer else got[level][s], flow[s], modules, step,
                        outer, after,
                    )
                    flow[s] = along(value, 0, step - 1 if level == 0 else line)
                elif step < line - 1:
                    if s == STREAMS - 1:
                        flow[s][0] = waiting[s][1][-1] = tie(flow[s][0], [hidden_new] + near[2][0] + far[2][0][:1] if step == 1 else near[2][0] + far[2][0][:1] + far[2][-1][:1])
                    flow[s] = along(flow[s], step, line)
                if step == 1 and level == 0:
                    first[1][s] = flow[s][:1]
                if waiting[s] is not None:
                    if step < line - 1:
                        waiting[s][1].append(flow[s][0])
                        waiting[s][2].append(flow[s][1])
                    if level < levels and step == max(line - 2, 1):
                        give(level - 1, s, tuple(range(line)), [])
                    if level == levels:
                        if step == max(line - 3, 1) and soon:
                            give(level - 1, s, tuple(soon), [hidden_new])
                        if step == max(line - 2, 1):
                            give(level - 1, s, tuple(late), [])
        if level < levels:
            for s in range(STREAMS):
                fresh, whole = update(
                    at_all[level], shares[level], own[level][s], got[level][s], flow[s], outer_weights, momentum, whole, level,
                    columns(level, s), [],
                )
                flow[s] = along((fresh, fresh), 0, line)
                waiting[s] = (fresh, [flow[s][0]], [flow[s][1]])
                if level == 0:
                    first[2][s] = flow[s][:1]
                if level == 2:
                    give(level, s, (0,), [])
        if level == 2:
            hidden_new = forward(
                hidden_kernel, order, hidden_table, inputs, (gate_new,), ring_parts(1), jnp.bfloat16, scale_d,
                line, block,
            )
        if level == 3:
            for s in range(STREAMS):
                parts = [part for pair in zip(near[2][s], far[2][s]) for part in pair]
                keep, send = down(high, hidden_new, parts, ranks, scale_f)
                outs.append(scatter_mp(keep, send, ranks, rank))

    outputs = jnp.concatenate(outs, axis=1).astype(jnp.bfloat16)
    return outputs, whole


def solution(mesh):
    return jax.shard_map(
        shards,
        mesh=mesh,
        in_specs=(
            P("path", "mp"),
            P("path", "mp"),
            P("path", None, "mp", None),
            P("path", None, None, "mp", None, None),
            P("path", None, None, "mp", None, None),
            P(),
            P(),
        ),
        out_specs=(P("path", "mp"), P("path", None, None, "mp", None, None)),
        check_vma=False,
    )
```

```python
import functools

import jax
import jax.numpy as jnp
from jax import lax
from jax.experimental import pallas as pl
from jax.experimental.pallas import tpu as pltpu
from jax.sharding import PartitionSpec as P

mu_outer = 0.9
eta_outer = 0.7
lr_inner = 2.0

STREAMS = 2
BRIEF = pl.CostEstimate(flops=1, bytes_accessed=1, transcendentals=0)
FOLD = 2


def contract(left, right, left_dim, right_dim):
    return lax.dot_general(
        left, right, (((left_dim,), (right_dim,)), ((), ())), preferred_element_type=jnp.float32
    )


def params(mib):
    return pltpu.CompilerParams(vmem_limit_bytes=mib * 2**20)


def spread(position, left, right_ref, chunks):
    size = left.shape[1] // chunks
    total = None
    for j in range(chunks):
        value = contract(left[:, j * size : (j + 1) * size], right_ref[position(j)], 1, 1)
        total = value if total is None else total + value
    return total


def open_kernel(scale, chunks, order_ref, x_ref, gate_w_ref, up_w_ref, gate_ref, up_ref):
    position = lambda j: order_ref[j]
    gate = spread(position, gate_w_ref[0, 0], x_ref, chunks) * scale
    upper = spread(position, up_w_ref[0, 0], x_ref, chunks) * scale
    gate_ref[...] = gate
    up_ref[...] = upper


def close_kernel(scale, chunks, order_ref, c_ref, weight_ref, gate_ref, up_ref, pre_gate_ref, pre_up_ref, hidden_ref):
    grad = spread(lambda j: order_ref[j], weight_ref[0, 0], c_ref, chunks) * scale
    gate, upper = gate_ref[...], up_ref[...]
    sig = jax.nn.sigmoid(gate)
    act = gate * sig
    pre_gate_ref[...] = (grad * upper * sig * (1.0 + gate * (1.0 - sig))).astype(jnp.bfloat16)
    pre_up_ref[...] = (grad * act).astype(jnp.bfloat16)
    hidden_ref[...] = (act * upper).astype(jnp.bfloat16)


def front(kernel, scale, order, right, weights, picked, extra, dtypes):
    chunks, rows, size = right.shape
    units, width = weights.shape[2:]
    tile = min(512, units)
    thin = pl.BlockSpec((tile, rows), lambda i, order: (i, 0))
    return pl.pallas_call(
        functools.partial(kernel, scale, chunks),
        grid_spec=pltpu.PrefetchScalarGridSpec(
            num_scalar_prefetch=1,
            grid=(units // tile,),
            in_specs=[pl.BlockSpec((chunks, rows, size), lambda i, order: (0, 0, 0))]
            + [
                pl.BlockSpec((1, 1, tile, width), lambda i, order, level=level: (0, level, i, 0))
                for level in picked
            ]
            + [thin] * len(extra),
            out_specs=[thin] * len(dtypes),
        ),
        out_shape=[jax.ShapeDtypeStruct((units, rows), dtype) for dtype in dtypes],
        compiler_params=params(16),
        cost_estimate=BRIEF,
    )(order, right, *[weights] * len(picked), *extra)


def tie(value, after):
    anywhere = pl.BlockSpec(memory_space=pl.ANY)
    return pl.pallas_call(
        lambda *refs: None,
        in_specs=[anywhere] * (1 + len(after)),
        out_specs=anywhere,
        out_shape=jax.ShapeDtypeStruct(value.shape, value.dtype),
        input_output_aliases={0: 0},
        compiler_params=params(1),
        cost_estimate=BRIEF,
    )(value, *after)


def finals_kernel(scale, block, pieces, split, table_ref, left_ref, right_ref, weight_ref, *refs):
    own_ref, send_refs = refs[0], refs[1:]
    line = own_ref.shape[0]
    grad = contract(left_ref[...], right_ref[0], 1, 0) * (lr_inner * scale)
    for q in range(pieces):
        rows = slice(q * block, (q + 1) * block)
        final = weight_ref[0, 0, rows, :].astype(jnp.float32) - grad[rows]
        spot = table_ref[1, q]
        leaves = table_ref[0, q] != 0
        outer = (spot == 0) | (spot == line - 1)

        @pl.when(jnp.logical_not(leaves))
        def _():
            own_ref[spot] = final

        if split:

            @pl.when(leaves & outer)
            def _():
                send_refs[0][jnp.where(spot == 0, 0, 1)] = final.astype(jnp.bfloat16)

            @pl.when(leaves & jnp.logical_not(outer))
            def _():
                send_refs[1][jnp.clip(spot - 1, 0, line - 3)] = final.astype(jnp.bfloat16)

        else:

            @pl.when(leaves)
            def _():
                send_refs[0][spot] = final.astype(jnp.bfloat16)


def finals(table, order, left, right, weights, level, columns, scale, line, block, split, after):
    start, tiles, tile = columns
    units, rows = left.shape
    per = right.shape[2] // tile
    width = tiles * tile
    counts = [line] + ([2, line - 2] if split else [line])

    def kernel(table_ref, order_ref, left_ref, right_ref, weight_ref, *refs):
        outs = refs[len(after) :]
        finals_kernel(scale, block, units // block, split, table_ref, left_ref, right_ref, weight_ref, *outs)

    return pl.pallas_call(
        kernel,
        grid_spec=pltpu.PrefetchScalarGridSpec(
            num_scalar_prefetch=2,
            grid=(tiles,),
            in_specs=[
                pl.BlockSpec((units, rows), lambda t, table, order: (0, 0)),
                pl.BlockSpec(
                    (1, rows, tile), lambda t, table, order: (order[start(t) // per], 0, start(t) % per)
                ),
                pl.BlockSpec((1, 1, units, tile), lambda t, table, order: (0, level, 0, start(t))),
            ]
            + [pl.BlockSpec(memory_space=pl.ANY)] * len(after),
            out_specs=[pl.BlockSpec((n, block, tile), lambda t, table, order: (0, 0, t)) for n in counts],
        ),
        out_shape=[
            jax.ShapeDtypeStruct((n, block, width), jnp.bfloat16 if i else jnp.float32)
            for i, n in enumerate(counts)
        ],
        compiler_params=params(16),
        cost_estimate=BRIEF,
    )(table, order, left, right, weights, *after)


def places(line, step):
    ups = lambda at: jnp.clip(line - step + at[2], 0, line - 1)
    downs = lambda at: jnp.clip(at[2] - line + step, 0, line - 1)
    return ups, downs


def running_kernel(line, step, flows, outs, at_ref, *refs):
    own_refs, got_refs, flow_refs, out_refs = refs[:2], refs[2:4], refs[4 : 4 + flows], refs[-outs:]
    modules = out_refs[0].shape[0]
    z = at_ref[2]
    lives = (z < step, z >= line - step)
    lower = 2 * z < line
    for m in range(modules):
        totals = []
        for way in range(2):
            total = jnp.where(lives[way] & (at_ref[0] == m), own_refs[way][0], 0.0)
            total = total + jnp.where(
                lives[way] & (at_ref[1] == m), got_refs[way][0].astype(jnp.float32), 0.0
            )
            if flows == 2:
                total = total + flow_refs[way][m].astype(jnp.float32)
            if flows == 1:
                mine = lower if way == 0 else jnp.logical_not(lower)
                total = total + jnp.where(mine, flow_refs[0][m].astype(jnp.float32), 0.0)
            totals.append(total)
        if outs == 1:
            totals = [jnp.where(lower, totals[0], totals[1])]
        for total, out_ref in zip(totals, out_refs):
            out_ref[m] = total.astype(jnp.bfloat16)


def running(at, own, got, flow, modules, step, outer, after):
    line, block, width = own.shape
    outs = 1 if not flow and line > 3 else 2
    tile = min(512, width)
    both = places(line, step)
    one = lambda spot: pl.BlockSpec((1, block, tile), lambda t, at: (spot(at), 0, t))
    ends = (lambda at: 1, lambda at: 0)
    wide = pl.BlockSpec((modules, block, tile), lambda t, at: (0, 0, t))
    return pl.pallas_call(
        functools.partial(running_kernel, line, step, len(flow), outs),
        grid_spec=pltpu.PrefetchScalarGridSpec(
            num_scalar_prefetch=1,
            grid=(width // tile,),
            in_specs=[one(spot) for spot in both]
            + [one(spot) for spot in (ends if outer else both)]
            + [wide] * len(flow)
            + [pl.BlockSpec(memory_space=pl.ANY)] * len(after),
            out_specs=[wide] * outs,
        ),
        out_shape=[jax.ShapeDtypeStruct((modules, block, width), jnp.bfloat16)] * outs,
        compiler_params=params(12),
        cost_estimate=BRIEF,
    )(at, own, own, got, got, *flow, *after)


def update_kernel(count, at_ref, share_ref, own_ref, got_ref, up_ref, low_ref, stored_ref, old_ref, *refs):
    fresh_ref, whole_ref = refs[-2:]
    for m in range(count):
        total = jnp.where(at_ref[0] == m, own_ref[0], 0.0)
        total = total + jnp.where(at_ref[1] == m, got_ref[0].astype(jnp.float32), 0.0)
        total = total + up_ref[m].astype(jnp.float32) + low_ref[m].astype(jnp.float32)
        stored = stored_ref[0, 0, m, 0]
        delta = stored - total / share_ref[m]
        velocity = mu_outer * old_ref[0, 0, m, 0].astype(jnp.float32) + delta
        fresh = (stored - eta_outer * (delta + mu_outer * velocity)).astype(jnp.bfloat16)
        fresh_ref[m] = fresh
        whole_ref[0, 0, m, 0] = fresh


def update(at, share, own, got, flow, outer_weights, momentum, whole, level, columns, after):
    start, tiles, tile = columns
    modules, block = outer_weights.shape[2], outer_weights.shape[4]
    one = pl.BlockSpec((1, block, tile), lambda t, at: (at[2], 0, t))
    wide = pl.BlockSpec((modules, block, tile), lambda t, at: (0, 0, t))
    state = pl.BlockSpec((1, 1, modules, 1, block, tile), lambda t, at: (0, level, 0, 0, 0, start(t)))
    extra = ([] if whole is None else [whole]) + after
    return pl.pallas_call(
        functools.partial(update_kernel, modules),
        grid_spec=pltpu.PrefetchScalarGridSpec(
            num_scalar_prefetch=1,
            grid=(tiles,),
            in_specs=[pl.BlockSpec(memory_space=pltpu.SMEM), one, one, wide, wide, state, state]
            + [pl.BlockSpec(memory_space=pl.ANY)] * len(extra),
            out_specs=[wide, state],
        ),
        out_shape=[
            jax.ShapeDtypeStruct((modules, block, tiles * tile), jnp.bfloat16),
            jax.ShapeDtypeStruct(outer_weights.shape, jnp.bfloat16),
        ],
        input_output_aliases={} if whole is None else {8: 1},
        compiler_params=params(16),
        cost_estimate=BRIEF,
    )(at, share, own, got, *flow, outer_weights, momentum, *extra)


def deliver_kernel(line, rings, at_ref, fresh_ref, *refs):
    ups, lows = refs[: len(rings)], refs[len(rings) : 2 * len(rings)]
    near_ref, far_ref, sems = refs[-3:]
    z = at_ref[2]
    for side, out_ref in enumerate((near_ref, far_ref)):
        module = at_ref[side]

        def copy(source, i, side=side, out_ref=out_ref, module=module):
            return pltpu.make_async_copy(source.at[module], out_ref.at[i], sems.at[side, i])

        for i, r in enumerate(rings):
            if r == 0:
                copy(fresh_ref, i).start()
                continue

            @pl.when(z >= r)
            def _():
                copy(ups[i], i).start()

            @pl.when(z < r)
            def _():
                copy(lows[i], i).start()

    for side, out_ref in enumerate((near_ref, far_ref)):
        for i in range(len(rings)):
            pltpu.make_async_copy(fresh_ref.at[0], out_ref.at[i], sems.at[side, i]).wait()


def deliver(at, fresh, ups, lows, line, rings, after):
    shape = jax.ShapeDtypeStruct((len(rings),) + fresh.shape[1:], fresh.dtype)
    anywhere = pl.BlockSpec(memory_space=pl.ANY)
    ups = [ups[r - 1] if r else fresh for r in rings]
    lows = [lows[line - 1 - r] if r else fresh for r in rings]
    return pl.pallas_call(
        functools.partial(deliver_kernel, line, rings),
        in_specs=[pl.BlockSpec(memory_space=pltpu.SMEM)] + [anywhere] * (2 * len(rings) + 1 + len(after)),
        out_specs=[pl.BlockSpec(memory_space=pltpu.VMEM)] * 2,
        out_shape=[shape, shape],
        scratch_shapes=[pltpu.SemaphoreType.DMA((2, len(rings)))],
        compiler_params=params(12),
        cost_estimate=BRIEF,
    )(at, fresh, *ups, *lows, *after)


def product(order_ref, x_ref, parts):
    total = None
    size = x_ref.shape[2]
    at = 0
    for part in parts:
        for i in range(part.shape[2] // size):
            left = part[:, :, i * size : (i + 1) * size].reshape(-1, size)
            value = contract(left, x_ref[order_ref[at]], 1, 1)
            total = value if total is None else total + value
            at += 1
    return total


def gate_kernel(scale, block, line, order_ref, table_ref, x_ref, *refs):
    out_ref = refs[-1]
    count = (len(refs) - 1) // 2
    for side, parts in enumerate((refs[:count], refs[count:-1])):
        value = product(order_ref, x_ref, parts) * scale
        for r in range(line):
            out_ref[table_ref[0, side * line + r]] = value[r * block : (r + 1) * block]


def hidden_kernel(scale, block, line, order_ref, table_ref, x_ref, gate_ref, *refs):
    out_ref = refs[-1]
    count = (len(refs) - 1) // 2
    for side, parts in enumerate((refs[:count], refs[count:-1])):
        value = product(order_ref, x_ref, parts) * scale
        for r in range(line):
            gate = gate_ref[table_ref[0, side * line + r]]
            upper = value[r * block : (r + 1) * block]
            hidden = gate * jax.nn.sigmoid(gate) * upper
            out_ref[table_ref[1, side * line + r]] = hidden.astype(jnp.bfloat16)


def forward(kernel, order, table, inputs, extra, parts, dtype, scale, line, block):
    chunks, rows, size = inputs.shape
    pieces = 2 * line
    smem = pl.BlockSpec(memory_space=pltpu.SMEM)
    vmem = pl.BlockSpec(memory_space=pltpu.VMEM)
    return pl.pallas_call(
        functools.partial(kernel, scale, block, line),
        in_specs=[smem, smem] + [vmem] * (1 + len(extra) + len(parts)),
        out_specs=vmem,
        out_shape=jax.ShapeDtypeStruct((pieces, block, rows), dtype),
        compiler_params=params(32),
        cost_estimate=BRIEF,
    )(order, table, inputs, *extra, *parts)


def down_kernel(scale, ranks, high_ref, left_ref, *refs):
    parts, keep_ref, send_ref = refs[:-2], refs[-2], refs[-1]
    rows = left_ref.shape[2]
    total = None
    at = 0
    for part in parts:
        count, block, width = part.shape
        left = left_ref[at : at + count].reshape(count * block, rows)
        value = contract(left, part[...].reshape(count * block, width), 0, 0)
        total = value if total is None else total + value
        at += count
    total = total * scale
    size = width // ranks
    high = high_ref[0] != 0
    for i in range(ranks // 2):
        low_part = total[:, 2 * i * size : (2 * i + 1) * size]
        high_part = total[:, (2 * i + 1) * size : (2 * i + 2) * size]
        spot = slice(i * size, (i + 1) * size)
        keep_ref[:, spot] = jnp.where(high, high_part, low_part)
        send_ref[:, spot] = jnp.where(high, low_part, high_part).astype(jnp.bfloat16)


def down(high, left, parts, ranks, scale):
    pieces, block, rows = left.shape
    width = parts[0].shape[2]
    vmem = pl.BlockSpec(memory_space=pltpu.VMEM)
    return pl.pallas_call(
        functools.partial(down_kernel, scale, ranks),
        in_specs=[pl.BlockSpec(memory_space=pltpu.SMEM)] + [vmem] * (1 + len(parts)),
        out_specs=[vmem] * 2,
        out_shape=[
            jax.ShapeDtypeStruct((rows, width // 2), jnp.float32),
            jax.ShapeDtypeStruct((rows, width // 2), jnp.bfloat16),
        ],
        compiler_params=params(24),
        cost_estimate=BRIEF,
    )(high, left, *parts)


def pairs_of(size, bit):
    return [(i, i ^ bit) for i in range(size)]


def gather_mp(values, size):
    held = [[value[None]] for value in values]
    offsets = [0]
    bit = size // 2
    while bit:
        held = [parts + [lax.ppermute(part, "mp", pairs_of(size, bit)) for part in parts] for parts in held]
        offsets = offsets + [offset ^ bit for offset in offsets]
        bit //= 2
    return held, offsets


def scatter_mp(keep, send, size, index):
    width = 2 * keep.shape[1] // size
    value = keep + lax.ppermute(send, "mp", pairs_of(size, 1)).astype(jnp.float32)
    bit = 2
    while bit < size:
        parts = [value[:, at : at + width] for at in range(0, value.shape[1], width)]
        high = (index & bit) != 0
        keep = [jnp.where(high, parts[i + 1], parts[i]) for i in range(0, len(parts), 2)]
        send = [jnp.where(high, parts[i], parts[i + 1]) for i in range(0, len(parts), 2)]
        got = lax.ppermute(jnp.concatenate(send, axis=1).astype(jnp.bfloat16), "mp", pairs_of(size, bit))
        value = jnp.concatenate(keep, axis=1) + got.astype(jnp.float32)
        bit *= 2
    return value


def shards(tokens, cotangent, path_weights, outer_weights, momentum, assignment, owners):
    paths = lax.axis_size("path")
    ranks = lax.axis_size("mp")
    line = paths // FOLD
    me = lax.axis_index("path")
    rank = lax.axis_index("mp")
    z, side = me // FOLD, me % FOLD
    levels, units, width = path_weights.shape[1:]
    modules, block = outer_weights.shape[2], outer_weights.shape[4]
    scale_d = width ** (-0.5)
    scale_f = (units * ranks) ** (-0.5)

    held, offsets = gather_mp([tokens, cotangent], ranks)
    inputs, upstream = (jnp.concatenate(parts, axis=0) for parts in held)
    spots = jnp.asarray([offsets.index(i) for i in range(ranks)], jnp.int32)
    rank_ids = jnp.arange(ranks, dtype=jnp.int32)
    order = jnp.sum(jnp.where((rank_ids ^ rank)[:, None] == rank_ids[None, :], spots[None, :], 0), axis=1)

    module_ids = jnp.arange(modules, dtype=jnp.int32)
    path_ids = jnp.arange(paths, dtype=jnp.int32)
    mine = lax.dynamic_index_in_dim(assignment, me, 1, keepdims=False)
    theirs = lax.dynamic_index_in_dim(assignment, me ^ 1, 1, keepdims=False)
    at_all = jnp.stack([mine, theirs, jnp.full_like(mine, z)], axis=1)
    is_mine = mine[:, None] == module_ids[None, :]
    shares = jnp.sum((assignment[:, None, :] == module_ids[None, :, None]).astype(jnp.float32), axis=2)
    owner_rows = jnp.sum(jnp.where(is_mine[:, :, None], owners, 0), axis=1)
    apart = (owner_rows % FOLD) ^ side
    leaves = jnp.stack([apart, owner_rows // FOLD], axis=1)
    slot = apart * line + (z - owner_rows // FOLD + line) % line
    piece_at = jnp.sum(
        jnp.where(slot[:, None, :] == path_ids[None, :, None], path_ids[None, None, :], 0), axis=2
    )
    down_at = jnp.sum(
        jnp.where(piece_at[1][:, None] == path_ids[None, :], slot[2][None, :], 0), axis=1
    )
    across = pairs_of(paths, 1)

    def permute(value, pairs):
        return lax.ppermute(value, "path", pairs)

    def along(values, first, last):
        up = [(i, i + FOLD) for i in range(paths - FOLD) if first <= i // FOLD <= last]
        low = [(paths - 1 - i, paths - 1 - j) for i, j in up]
        if len(values) == 1:
            return [permute(values[0], up + low)]
        return [permute(values[0], up), permute(values[1], low)]

    half = width // STREAMS
    chunk = width // ranks
    narrow = chunk // STREAMS

    def columns(level, s):
        if level == 2:
            return (lambda t: t * STREAMS + s), ranks, narrow
        tile = min(chunk, half)
        return (lambda t: s * (half // tile) + t), half // tile, tile

    gate, upper = front(
        open_kernel, scale_d, order, inputs, path_weights, (0, 1), (), (jnp.float32, jnp.float32)
    )
    pre_gate, pre_up, hidden = front(
        close_kernel, scale_f, order, upstream, path_weights, (2,), (gate, upper), (jnp.bfloat16,) * 3
    )
    sources = ((pre_gate, inputs, scale_d), (pre_up, inputs, scale_d), (hidden, upstream, scale_f))

    late = [r for r in range(line) if max(r - 1, line - 1 - r) == line - 2 and r]
    soon = [r for r in range(1, line) if r not in late]
    parts_of = [(side, r) for rings in ([0], soon, late) for side in range(FOLD) for r in rings]
    turn = jnp.asarray([parts_of.index((e // line, e % line)) for e in range(paths)], jnp.int32)
    down_at = jnp.sum(jnp.where(down_at[:, None] == path_ids[None, :], turn[None, :], 0), axis=1)
    gate_table = piece_at[0][None]
    hidden_table = jnp.stack([piece_at[1], down_at])
    high = (rank & 1)[None]

    flow = [[] for _ in range(STREAMS)]
    first = [[[] for _ in range(STREAMS)] for _ in range(levels)]
    waiting = [None] * STREAMS
    near = [[[] for _ in range(STREAMS)] for _ in range(levels)]
    far = [[[] for _ in range(STREAMS)] for _ in range(levels)]
    whole = None
    hidden_new = gate_new = None

    def give(level, s, rings, after):
        fresh, ups, lows = waiting[s]
        held, leaving = deliver(at_all[level], fresh, ups, lows, line, rings, after)
        near[level][s].append(held)
        far[level][s].append(permute(leaving, across))

    def ring_parts(level):
        return [part for half in (near, far) for s in range(STREAMS) for part in half[level][s]]

    own = [[None] * STREAMS for _ in range(levels)]
    got = [[None] * STREAMS for _ in range(levels)]
    ends = [None] * STREAMS

    def prepare(level):
        left, right, scale = sources[level]
        for s in range(STREAMS):
            own[level][s], *sent = finals(
                leaves[level], order, left, right, path_weights, level, columns(level, s), scale, line, block,
                level == 0 and line > 2, first[level][s],
            )
            if len(sent) > 1:
                ends[s] = permute(sent[0], across)
                middle = permute(sent[1], across)
                got[level][s] = jnp.concatenate([ends[s][:1], middle, ends[s][1:]], axis=0)
            else:
                got[level][s] = permute(sent[0], across)

    outs = []
    for level in range(levels + 1):
        if level == 0:
            prepare(0)
        if level == 1:
            prepare(1)
            prepare(2)
        if level == 2:
            gate_new = forward(
                gate_kernel, order, gate_table, inputs, (), ring_parts(0), jnp.float32, scale_d, line, block
            )
        for step in range(1, line):
            for s in range(STREAMS):
                if level < levels:
                    outer = level == 0 and line > 2 and step == 1
                    after = near[level - 1][s] if level and step == line - 1 else []
                    if level == 1 and step == line - 1:
                        after = after + [got[2][s]]
                    if level == 2 and step == line - 2 and s == 0:
                        after = after + [gate_new]
                    value = running(
                        at_all[level], own[level][s], ends[s] if outer else got[level][s], flow[s], modules, step,
                        outer, after,
                    )
                    flow[s] = along(value, 0, step - 1 if level == 0 else line)
                elif step < line - 1:
                    if s == STREAMS - 1:
                        flow[s][0] = waiting[s][1][-1] = tie(flow[s][0], [hidden_new] + near[2][0] + far[2][0][:1] if step == 1 else near[2][0] + far[2][0][:1] + far[2][-1][:1])
                    flow[s] = along(flow[s], step, line)
                if step == 1 and level == 0:
                    first[1][s] = flow[s][:1]
                if waiting[s] is not None:
                    if step < line - 1:
                        waiting[s][1].append(flow[s][0])
                        waiting[s][2].append(flow[s][1])
                    if level < levels and step == max(line - 2, 1):
                        give(level - 1, s, tuple(range(line)), [])
                    if level == levels:
                        if step == max(line - 3, 1) and soon:
                            give(level - 1, s, tuple(soon), [hidden_new])
                        if step == max(line - 2, 1):
                            give(level - 1, s, tuple(late), [])
        if level < levels:
            for s in range(STREAMS):
                fresh, whole = update(
                    at_all[level], shares[level], own[level][s], got[level][s], flow[s], outer_weights, momentum, whole, level,
                    columns(level, s), [],
                )
                flow[s] = along((fresh, fresh), 0, line)
                waiting[s] = (fresh, [flow[s][0]], [flow[s][1]])
                if level == 0:
                    first[2][s] = flow[s][:1]
                if level == 2:
                    give(level, s, (0,), [])
        if level == 2:
            hidden_new = forward(
                hidden_kernel, order, hidden_table, inputs, (gate_new,), ring_parts(1), jnp.bfloat16, scale_d,
                line, block,
            )
        if level == 3:
            for s in range(STREAMS):
                parts = [part for pair in zip(near[2][s], far[2][s]) for part in pair]
                keep, send = down(high, hidden_new, parts, ranks, scale_f)
                outs.append(scatter_mp(keep, send, ranks, rank))

    outputs = jnp.concatenate(outs, axis=1).astype(jnp.bfloat16)
    return outputs, whole


def solution(mesh):
    return jax.shard_map(
        shards,
        mesh=mesh,
        in_specs=(
            P("path", "mp"),
            P("path", "mp"),
            P("path", None, "mp", None),
            P("path", None, None, "mp", None, None),
            P("path", None, None, "mp", None, None),
            P(),
            P(),
        ),
        out_specs=(P("path", "mp"), P("path", None, None, "mp", None, None)),
        check_vma=False,
    )
```
